32 devices in a mesh: energy: 4 (over y, x), cell: 8 (over z, core).
Axes of the slice: x: 2, y: 2, z: 4, core: 2. Of those that a mesh axis runs over, the one named last changes fastest.
Arguments:
- green_less: float32 [2, 4, 8, 320, 320], P(None, None, 'cell', 'energy'), may hold values from -6 to 6
- green_greater: float32 [2, 4, 8, 320, 320], P(None, None, 'cell', 'energy'), may hold values from -6 to 6
- offsets: int32 [4], replicated, may hold values from 0 to 3, as said below
- orbitals: int32 [8], replicated, may hold values from 192 to 320
- coulomb_diag: float32 [8, 320, 320], P('cell'), may hold values from -0.3125 to 0.3125
- coulomb_up: float32 [8, 320, 320], P('cell'), may hold values from -0.3125 to 0.3125
Outputs:
- screened_diag: float32 [2, 4, 8, 320, 320], P(None, 'energy', 'cell')
- screened_up: float32 [2, 4, 8, 320, 320], P(None, 'energy', 'cell')
The draws below stay inside these ranges and needn't reach their ends.
Inputs may be any that keep to these rules, and one draw needn't show every extreme that they name: offsets is a permutation of 0 to 3.
All inputs are finite; a program needn't handle non-finite values.
Results may differ from the reference program's by a relative error of at most 0.0003.
Values sent between devices are 32-bit elements; how exact they have to be, the bound alone decides.
A program may use at most 64 MiB of HBM per device.

```python
import math
import jax
import jax.numpy as jnp
from jax import lax

BLK = 320
NE = 4
NC = 8


def draw_offsets(key, part):
    return jax.random.permutation(key, NE).astype(jnp.int32)


def place_ends(entries, key, smallest, largest):
    dims = entries.shape
    spot = [jax.random.randint(jax.random.fold_in(key, axis), (), 0, dims[axis]) for axis in range(len(dims))]
    entries = entries.at[tuple(spot)].set(smallest)
    longest = dims.index(max(dims))
    spot[longest] = (spot[longest] + 1) % dims[longest]
    return entries.at[tuple(spot)].set(largest)


def levels(rng, extent, cuts, low, high):
    level = 1.0
    for position, shards_of in cuts:
        heights = jax.random.uniform(jax.random.fold_in(jax.random.fold_in(rng, 6), position), (shards_of,), jnp.float32, low / len(cuts), high / len(cuts))
        level = level * jnp.repeat(jnp.exp(heights), extent[position] // shards_of).reshape((-1,) + (1,) * (len(extent) - 1 - position))
    return level


def scatter_about(own_key, extent, deviation, limit, cuts=(), kind=jnp.bfloat16):
    drawn = deviation * jax.random.normal(own_key, extent, jnp.float32)
    if cuts:
        drawn = drawn * levels(own_key, extent, cuts, -0.22, 0.18)
    return jnp.clip(drawn, -limit, limit).astype(kind)


def setup_inputs(seed: int = 0) -> dict:
    streams_of = jax.random.split(jax.random.key(seed), 7)
    return {
        "green_less": scatter_about(streams_of[0], (2, NE, NC, BLK, BLK), 1.0, 6.0, ((2, 8), (3, 4)), jnp.float32),
        "green_greater": scatter_about(streams_of[1], (2, NE, NC, BLK, BLK), 1.0, 6.0, ((2, 8), (3, 4)), jnp.float32),
        "offsets": draw_offsets(jax.random.fold_in(streams_of[6], 71), 0),
        "orbitals": place_ends(jax.random.randint(streams_of[3], (NC,), 3 * BLK // 5, BLK + 1), jax.random.fold_in(streams_of[3], 1), 3 * BLK // 5, BLK).astype(jnp.int32),
        "coulomb_diag": scatter_about(streams_of[4], (NC, BLK, BLK), BLK ** -0.5, 0.3125, ((0, 8),), jnp.float32),
        "coulomb_up": scatter_about(streams_of[5], (NC, BLK, BLK), BLK ** -0.5, 0.3125, ((0, 8),), jnp.float32),
    }


HIGH = lax.Precision.HIGHEST

def polarize(lesser, greater, offsets):
    count = lesser.shape[1]
    energies = jnp.arange(count, dtype=jnp.int32)

    def single(shift):
        source = energies - shift
        weight = (source >= 0).astype(jnp.float32)
        picked = jnp.take(greater, jnp.clip(source, 0, count - 1).astype(jnp.int32), axis=1)
        real_part = lesser[0] * picked[0] + lesser[1] * picked[1]
        imag_part = lesser[1] * picked[0] - lesser[0] * picked[1]
        weight = weight.reshape((count,) + (1,) * (lesser.ndim - 2))
        return jnp.stack([lax.optimization_barrier(jnp.sum(real_part * weight, axis=0)), lax.optimization_barrier(jnp.sum(imag_part * weight, axis=0))])
    return lax.map(single, offsets) / math.sqrt(count)

def left_mul(coupling, blocks):
    return jnp.einsum('cij,xcjk->xcik', coupling, blocks, precision=HIGH)

def left_mul_t(coupling, blocks):
    return jnp.einsum('cji,xcjk->xcik', coupling, blocks, precision=HIGH)

def right_mul(blocks, coupling):
    return jnp.einsum('xcij,cjk->xcik', blocks, coupling, precision=HIGH)

def right_mul_t(blocks, coupling):
    return jnp.einsum('xcij,ckj->xcik', blocks, coupling, precision=HIGH)

def screen(polar, vdiag, vup):
    zero_cell = jnp.zeros_like(polar[:, :1])
    zero_block = jnp.zeros_like(vdiag[:1])
    prev_polar = jnp.concatenate([zero_cell, polar[:, :-1]], axis=1)
    next_polar = jnp.concatenate([polar[:, 1:], zero_cell], axis=1)
    prev_up = jnp.concatenate([zero_block, vup[:-1]], axis=0)
    next_diag = jnp.concatenate([vdiag[1:], zero_block], axis=0)
    cells = vdiag.shape[0]
    keep = (jnp.arange(cells, dtype=jnp.int32) < cells - 1).astype(jnp.float32).reshape(1, cells, 1, 1)
    a_here = left_mul(vdiag, polar)
    a_next = left_mul(vup, next_polar)
    diag = right_mul_t(a_here, vdiag) + right_mul_t(a_next, vup) + right_mul(left_mul_t(prev_up, prev_polar), prev_up)
    upper = right_mul(a_here, vup) * keep + right_mul_t(a_next, next_diag)
    return (diag, upper)

def reference(green_less, green_greater, offsets, orbitals, coulomb_diag, coulomb_up):
    rows = jnp.arange(BLK, dtype=jnp.int32)
    inside = (rows[None, :] < orbitals[:, None]).astype(jnp.float32)
    inside_next = (rows[None, :] < jnp.roll(orbitals, -1)[:, None]).astype(jnp.float32)
    vdiag = coulomb_diag * inside[:, :, None] * inside[:, None, :]
    vup = coulomb_up * inside[:, :, None] * inside_next[:, None, :]
    polar = polarize(green_less, green_greater, offsets)

    def per_energy(blocks):
        return screen(blocks, vdiag, vup)
    diag, upper = lax.map(per_energy, polar)
    return (jnp.moveaxis(diag, 0, 1), jnp.moveaxis(upper, 0, 1))
```

```python
import functools
import math

import jax
import jax.numpy as jnp
from jax import lax
from jax.experimental import pallas as pl
from jax.experimental.pallas import tpu as pltpu
from jax.sharding import PartitionSpec as P

MESH = pl.DeviceIdType.MESH
F32 = jnp.float32
BF16 = jnp.bfloat16
HERE, NEXT, PREV = 0, 1, 2


def pack(first, second, main):
    return jnp.concatenate(
        [first[:, :main], second[:, :main], first[:, main:], second[:, main:]], axis=1
    )


def unpack(both, main, width):
    edge = 2 * main + width - main
    first = jnp.concatenate([both[:, :main], both[:, 2 * main:edge]], axis=1)
    second = jnp.concatenate([both[:, main:2 * main], both[:, edge:]], axis=1)
    return first, second


def halves(x):
    high = x.astype(BF16).astype(F32)
    return high, x - high


def lane_pad(parts):
    total = sum(p.shape[1] for p in parts)
    extra = -total % 128
    if extra:
        parts = parts + [jnp.zeros((parts[0].shape[0], extra), F32)]
    return jnp.concatenate(parts, axis=1).astype(BF16)


def row_pad(parts):
    total = sum(p.shape[0] for p in parts)
    extra = -total % 128
    if extra:
        parts = parts + [jnp.zeros((extra, parts[0].shape[1]), F32)]
    return jnp.concatenate(parts, axis=0).astype(BF16)


def left_operand(block):
    high, low = halves(block)
    return lane_pad([high, low, high])


def left_rows(rows):
    high, low = halves(rows)
    return row_pad([high, high, low])


def right_operand(main, tail):
    high, low = halves(main)
    end_high, end_low = halves(tail)
    return jnp.concatenate(
        [high.astype(BF16), low.astype(BF16), high.astype(BF16), lane_pad([end_high, end_low, end_high])],
        axis=1,
    )


def right_rows(block, main):
    high, low = halves(block)
    return row_pad(
        [high[:main], high[:main], low[:main], high[main:], high[main:], low[main:]]
    )


def dot(a, b):
    return jnp.dot(a, b, preferred_element_type=F32)


def kernel(
    energies, cells, offsets, orbitals, less_hbm, greater_hbm, vdiag_hbm, vup_hbm,
    diag_hbm, upper_hbm,
    less, greater, vdiag, vup, shifted, outgoing, polar, beside, v_out, v_in,
    left, right, right_prev, a_sum, o_sum, diag, upper,
    in_sem, out_sem, swap_send, swap_recv, side_send, side_recv, v_send, v_recv,
):
    me = lax.axis_index("energy")
    cell = lax.axis_index("cell")
    rows, width = less.shape[2], less.shape[3]
    main = width // 128 * 128
    half = width // 2
    has_next = cell < cells - 1
    has_prev = cell > 0

    def peer(k):
        if energies & (energies - 1):
            return lax.rem(me + k, energies)
        other, bit = me, 1
        while bit <= k:
            if k & bit:
                other = other + bit * (1 - 2 * lax.rem(me // bit, 2))
            bit *= 2
        return other

    loads = [
        pltpu.make_async_copy(src, dst, in_sem.at[i])
        for i, (src, dst) in enumerate(
            [(vdiag_hbm, vdiag), (vup_hbm, vup), (less_hbm, less), (greater_hbm, greater)]
        )
    ]
    for load in loads:
        load.start()

    barrier = pltpu.get_barrier_semaphore()
    for k in range(1, energies):
        pl.semaphore_signal(barrier, inc=1, device_id=(peer(k), cell), device_id_type=MESH)

    @pl.when(has_next)
    def _():
        pl.semaphore_signal(barrier, inc=1, device_id=(me, cell + 1), device_id_type=MESH)

    @pl.when(has_prev)
    def _():
        pl.semaphore_signal(barrier, inc=1, device_id=(me, cell - 1), device_id_type=MESH)

    @pl.when(jnp.logical_not(has_prev))
    def _():
        beside[0] = jnp.zeros(beside.shape[1:], F32)
        v_in[0] = jnp.zeros(v_in.shape[1:], F32)

    @pl.when(jnp.logical_not(has_next))
    def _():
        beside[1] = jnp.zeros(beside.shape[1:], F32)
        v_in[1] = jnp.zeros(v_in.shape[1:], F32)

    def v_copy(side):
        return pltpu.make_async_remote_copy(
            src_ref=v_out.at[side], dst_ref=v_in.at[side],
            send_sem=v_send.at[side], recv_sem=v_recv.at[side],
            device_id=(me, cell + 1 - 2 * side), device_id_type=MESH,
        )

    def side_copy(side, slot):
        return pltpu.make_async_remote_copy(
            src_ref=polar.at[slot], dst_ref=beside.at[side, slot],
            send_sem=side_send.at[side, slot], recv_sem=side_recv.at[side, slot],
            device_id=(me, cell + 1 - 2 * side), device_id_type=MESH,
        )

    def swap_copy(k):
        return pltpu.make_async_remote_copy(
            src_ref=outgoing.at[peer(k)], dst_ref=polar.at[me],
            send_sem=swap_send.at[k], recv_sem=swap_recv.at[k],
            device_id=(peer(k), cell), device_id_type=MESH,
        )

    def swap_arrival(k):
        back = k if not energies & (energies - 1) else energies - k
        return pltpu.make_async_remote_copy(
            src_ref=outgoing.at[peer(back)], dst_ref=polar.at[peer(back)],
            send_sem=swap_send.at[k], recv_sem=swap_recv.at[k],
            device_id=(peer(back), cell), device_id_type=MESH,
        ), peer(back)

    def forward(slot):
        @pl.when(has_next)
        def _():
            side_copy(0, slot).start()

        @pl.when(has_prev)
        def _():
            side_copy(1, slot).start()

    here_orbitals = orbitals[cell]
    next_orbitals = jnp.where(has_next, orbitals[jnp.minimum(cell + 1, cells - 1)], 0)
    row = lax.broadcasted_iota(jnp.int32, (width, width), 0)
    col = lax.broadcasted_iota(jnp.int32, (width, width), 1)
    loads[0].wait()
    loads[1].wait()
    vd = jnp.where((row < here_orbitals) & (col < here_orbitals), vdiag[...], 0.0)
    vu = jnp.where((row < here_orbitals) & (col < next_orbitals), vup[...], 0.0)
    vdiag[...] = vd
    vup[...] = vu
    v_out[0] = pack(vu[:half], vu[half:], main)
    v_out[1] = pack(vd[:half], vd[half:], main)

    met = energies - 1 + jnp.where(has_next, 1, 0) + jnp.where(has_prev, 1, 0)
    pl.semaphore_wait(barrier, met)

    @pl.when(has_next)
    def _():
        v_copy(0).start()

    @pl.when(has_prev)
    def _():
        v_copy(1).start()

    loads[2].wait()
    loads[3].wait()
    scale = 1.0 / math.sqrt(energies)

    def polarize(step, carry):
        at = pl.ds(pl.multiple_of(step * 8, 8), 8)
        l_re = [less[0, m, at, :] for m in range(energies)]
        l_im = [less[1, m, at, :] for m in range(energies)]
        g_re = [greater[0, m, at, :] for m in range(energies)]
        g_im = [greater[1, m, at, :] for m in range(energies)]
        for shift in range(energies):
            real = imag = None
            for m in range(shift, energies):
                r = l_re[m] * g_re[m - shift] + l_im[m] * g_im[m - shift]
                i = l_im[m] * g_re[m - shift] - l_re[m] * g_im[m - shift]
                real = r if real is None else real + r
                imag = i if imag is None else imag + i
            shifted[shift, at, :] = pack(real * scale, imag * scale, main)
        return carry

    lax.fori_loop(0, rows // 8, polarize, 0)
    for k in reversed(range(1, energies)):
        n = peer(k)
        outgoing[n] = shifted[offsets[n]]
        swap_copy(k).start()
    polar[me] = shifted[offsets[me]]
    forward(me)

    def cut(which, block):
        for e in range(energies):
            left[which, e] = left_operand(block[:, e * rows:(e + 1) * rows])

    vd = vdiag[...]
    cut(HERE, vd)
    right[HERE] = right_rows(pack(vd.T, vup[...], main), main)
    vu = vup[...]
    cut(NEXT, vu)

    def add_left(which, slot, block, first):
        product = dot(left[which, slot], left_rows(block))
        if first:
            a_sum[which] = product
        else:
            a_sum[which] += product

    def split(which):
        a = a_sum[which]
        edge = 2 * main + width - main
        return (
            right_operand(a[:, :main], a[:, 2 * main:edge]),
            right_operand(a[:, main:2 * main], a[:, edge:]),
        )

    def arrive(k):
        copy, slot = swap_arrival(k)
        copy.wait_recv()
        forward(slot)
        return slot

    slots = [me]

    def take_here(k):
        if k:
            slots.append(arrive(k))
        add_left(HERE, slots[k], polar[slots[k]], k == 0)

    def take_sides(k):
        slot = slots[k]

        @pl.when(has_prev)
        def _():
            side_copy(0, slot).wait_recv()

        @pl.when(has_next)
        def _():
            side_copy(1, slot).wait_recv()

        add_left(PREV, slot, beside[0, slot], k == 0)
        add_left(NEXT, slot, beside[1, slot], k == 0)

    take_here(0)
    early = max(1, energies - 1)
    for k in range(1, early):
        take_here(k)

    @pl.when(has_prev)
    def _():
        v_copy(0).wait_recv()

    @pl.when(has_next)
    def _():
        v_copy(1).wait_recv()

    def whole(packed):
        top, bottom = unpack(packed, main, width)
        return jnp.concatenate([top, bottom], axis=0)

    vp = whole(v_in[0])
    cut(PREV, vp.T)
    right_prev[...] = right_rows(
        jnp.concatenate([vp, jnp.zeros((width, -width % 128), F32)], axis=1), main
    )
    vn = whole(v_in[1])
    right[NEXT] = right_rows(pack(vup[...].T, vn.T, main), main)

    for k in range(early - 1):
        take_sides(k)
    for k in range(early, energies):
        take_here(k)
    for part, operand in enumerate(split(HERE)):
        o_sum[part] = dot(operand, right[HERE])
    for k in range(early - 1, energies):
        take_sides(k)
    for part, (after, before) in enumerate(zip(split(NEXT), split(PREV))):
        total = o_sum[part] + dot(after, right[NEXT])
        from_prev = dot(before, right_prev[...])
        first, second = unpack(total, main, width)
        diag[part] = first + from_prev[:, :width]
        upper[part] = second
        pltpu.make_async_copy(diag.at[part], diag_hbm.at[part], out_sem.at[0, part]).start()
        pltpu.make_async_copy(upper.at[part], upper_hbm.at[part], out_sem.at[1, part]).start()

    for k in range(1, energies):
        swap_copy(k).wait_send()

    @pl.when(has_next)
    def _():
        v_copy(0).wait_send()
        for slot in range(energies):
            side_copy(0, slot).wait_send()

    @pl.when(has_prev)
    def _():
        v_copy(1).wait_send()
        for slot in range(energies):
            side_copy(1, slot).wait_send()

    for part in range(2):
        pltpu.make_async_copy(diag.at[part], diag_hbm.at[part], out_sem.at[0, part]).wait()
        pltpu.make_async_copy(upper.at[part], upper_hbm.at[part], out_sem.at[1, part]).wait()


def solution(mesh):
    energies, cells = mesh.shape["energy"], mesh.shape["cell"]

    def per_device(green_less, green_greater, offsets, orbitals, coulomb_diag, coulomb_up):
        less = jnp.squeeze(green_less, 2)
        greater = jnp.squeeze(green_greater, 2)
        rows, width = less.shape[2], less.shape[3]
        main = width // 128 * 128
        depth = 3 * rows + -3 * rows % 128
        long = 3 * width + -3 * width % 128
        shape = jax.ShapeDtypeStruct((2, width, width), F32)
        anywhere = pl.BlockSpec(memory_space=pl.ANY)
        scalars = pl.BlockSpec(memory_space=pltpu.SMEM)
        dma = pltpu.SemaphoreType.DMA
        products = width * width * width * 2 * 8 * 3
        diag, upper = pl.pallas_call(
            functools.partial(kernel, energies, cells),
            out_shape=(shape, shape),
            in_specs=[scalars, scalars, anywhere, anywhere, anywhere, anywhere],
            out_specs=(anywhere, anywhere),
            scratch_shapes=[
                pltpu.VMEM(less.shape, F32),
                pltpu.VMEM(less.shape, F32),
                pltpu.VMEM((width, width), F32),
                pltpu.VMEM((width, width), F32),
                pltpu.VMEM((energies, rows, 2 * width), F32),
                pltpu.VMEM((energies, rows, 2 * width), F32),
                pltpu.VMEM((energies, rows, 2 * width), F32),
                pltpu.VMEM((2, energies, rows, 2 * width), F32),
                pltpu.VMEM((2, width // 2, 2 * width), F32),
                pltpu.VMEM((2, width // 2, 2 * width), F32),
                pltpu.VMEM((3, energies, width, depth), BF16),
                pltpu.VMEM((2, long, 2 * width), BF16),
                pltpu.VMEM((long, width + -width % 128), BF16),
                pltpu.VMEM((3, width, 2 * width), F32),
                pltpu.VMEM((2, width, 2 * width), F32),
                pltpu.VMEM((2, width, width), F32),
                pltpu.VMEM((2, width, width), F32),
                dma((4,)),
                dma((2, 2)),
                dma((energies,)),
                dma((energies,)),
                dma((2, energies)),
                dma((2, energies)),
                dma((2,)),
                dma((2,)),
            ],
            compiler_params=pltpu.CompilerParams(
                collective_id=0, has_side_effects=True, vmem_limit_bytes=48 * 1024 * 1024
            ),
            cost_estimate=pl.CostEstimate(
                flops=2 * products, bytes_accessed=4 * less.size * 4, transcendentals=0
            ),
            name="screen",
        )(offsets, orbitals, less, greater, coulomb_diag[0], coulomb_up[0])
        return diag[:, None, None], upper[:, None, None]

    in_specs = (
        P(None, None, "cell", "energy", None),
        P(None, None, "cell", "energy", None),
        P(),
        P(),
        P("cell", None, None),
        P("cell", None, None),
    )
    out_specs = (P(None, "energy", "cell", None, None), P(None, "energy", "cell", None, None))
    return jax.shard_map(
        per_device, mesh=mesh, in_specs=in_specs, out_specs=out_specs, check_vma=False
    )
```

```python
import functools
import math

import jax
import jax.numpy as jnp
from jax import lax
from jax.experimental import pallas as pl
from jax.experimental.pallas import tpu as pltpu
from jax.sharding import PartitionSpec as P

MESH = pl.DeviceIdType.MESH
F32 = jnp.float32
BF16 = jnp.bfloat16
HERE, NEXT, PREV = 0, 1, 2


def pack(first, second, main):
    return jnp.concatenate(
        [first[:, :main], second[:, :main], first[:, main:], second[:, main:]], axis=1
    )


def unpack(both, main, width):
    edge = 2 * main + width - main
    first = jnp.concatenate([both[:, :main], both[:, 2 * main:edge]], axis=1)
    second = jnp.concatenate([both[:, main:2 * main], both[:, edge:]], axis=1)
    return first, second


def halves(x):
    high = x.astype(BF16).astype(F32)
    return high, x - high


def lane_pad(parts):
    total = sum(p.shape[1] for p in parts)
    extra = -total % 128
    if extra:
        parts = parts + [jnp.zeros((parts[0].shape[0], extra), F32)]
    return jnp.concatenate(parts, axis=1).astype(BF16)


def row_pad(parts):
    total = sum(p.shape[0] for p in parts)
    extra = -total % 128
    if extra:
        parts = parts + [jnp.zeros((extra, parts[0].shape[1]), F32)]
    return jnp.concatenate(parts, axis=0).astype(BF16)


def left_operand(block):
    high, low = halves(block)
    return lane_pad([high, low, high])


def left_rows(rows):
    high, low = halves(rows)
    return row_pad([high, high, low])


def right_operand(main, tail):
    high, low = halves(main)
    end_high, end_low = halves(tail)
    return jnp.concatenate(
        [high.astype(BF16), low.astype(BF16), high.astype(BF16), lane_pad([end_high, end_low, end_high])],
        axis=1,
    )


def right_rows(block, main):
    high, low = halves(block)
    return row_pad(
        [high[:main], high[:main], low[:main], high[main:], high[main:], low[main:]]
    )


def dot(a, b):
    return jnp.dot(a, b, preferred_element_type=F32)


def kernel(
    energies, cells, offsets, orbitals, less_hbm, greater_hbm, vdiag_hbm, vup_hbm,
    diag, upper,
    less, greater, vdiag, vup, shifted, outgoing, polar, beside, v_out, v_in,
    left, right, a_sum, o_sum,
    in_sem, swap_send, swap_recv, side_send, side_recv, v_send, v_recv, trade_send,
):
    me = lax.axis_index("energy")
    cell = lax.axis_index("cell")
    rows, width = less.shape[2], less.shape[3]
    main = width // 128 * 128
    half = width // 2
    has_next = cell < cells - 1
    has_prev = cell > 0

    def peer(k):
        if energies & (energies - 1):
            return lax.rem(me + k, energies)
        other, bit = me, 1
        while bit <= k:
            if k & bit:
                other = other + bit * (1 - 2 * lax.rem(me // bit, 2))
            bit *= 2
        return other

    loads = [
        pltpu.make_async_copy(src, dst, in_sem.at[i])
        for i, (src, dst) in enumerate(
            [(vdiag_hbm, vdiag), (vup_hbm, vup), (less_hbm, less), (greater_hbm, greater)]
        )
    ]
    for load in loads:
        load.start()

    barrier = pltpu.get_barrier_semaphore()
    for k in range(1, energies):
        pl.semaphore_signal(barrier, inc=1, device_id=(peer(k), cell), device_id_type=MESH)

    @pl.when(has_next)
    def _():
        pl.semaphore_signal(barrier, inc=1, device_id=(me, cell + 1), device_id_type=MESH)

    @pl.when(has_prev)
    def _():
        pl.semaphore_signal(barrier, inc=1, device_id=(me, cell - 1), device_id_type=MESH)

    @pl.when(jnp.logical_not(has_prev))
    def _():
        beside[0] = jnp.zeros(beside.shape[1:], F32)
        v_in[0] = jnp.zeros(v_in.shape[1:], F32)

    @pl.when(jnp.logical_not(has_next))
    def _():
        beside[1] = jnp.zeros(beside.shape[1:], F32)
        v_in[1] = jnp.zeros(v_in.shape[1:], F32)

    odd = lax.rem(cell, 2)
    trading = energies % 4 == 0
    trader = peer(1) * (1 - odd) + peer(2) * odd

    def half_of(side):
        return lax.rem(me, 2) if side == 0 else lax.rem(me // 2, 2)

    def v_copy(side, part):
        return pltpu.make_async_remote_copy(
            src_ref=v_out.at[side, part], dst_ref=v_in.at[side, part],
            send_sem=v_send.at[side, part], recv_sem=v_recv.at[side, part],
            device_id=(me, cell + 1 - 2 * side), device_id_type=MESH,
        )

    def trade_copy(side, part):
        return pltpu.make_async_remote_copy(
            src_ref=v_in.at[side, part], dst_ref=v_in.at[side, part],
            send_sem=trade_send, recv_sem=v_recv.at[side, part],
            device_id=(trader, cell), device_id_type=MESH,
        )

    def each_v(act):
        for side, there in ((0, has_next), (1, has_prev)):
            if not trading:
                @pl.when(there)
                def _():
                    act(v_copy(side, 0))
                    act(v_copy(side, 1))
                continue
            crosses = odd == 1 - side

            @pl.when(there & crosses)
            def _():
                act(v_copy(side, half_of(side)))

            @pl.when(there & jnp.logical_not(crosses))
            def _():
                act(v_copy(side, 0))
                act(v_copy(side, 1))

    def side_copy(side, slot):
        return pltpu.make_async_remote_copy(
            src_ref=polar.at[slot], dst_ref=beside.at[side, slot],
            send_sem=side_send.at[side, slot], recv_sem=side_recv.at[side, slot],
            device_id=(me, cell + 1 - 2 * side), device_id_type=MESH,
        )

    def swap_copy(k):
        return pltpu.make_async_remote_copy(
            src_ref=outgoing.at[peer(k)], dst_ref=polar.at[me],
            send_sem=swap_send.at[k], recv_sem=swap_recv.at[k],
            device_id=(peer(k), cell), device_id_type=MESH,
        )

    def swap_arrival(k):
        back = k if not energies & (energies - 1) else energies - k
        return pltpu.make_async_remote_copy(
            src_ref=outgoing.at[peer(back)], dst_ref=polar.at[peer(back)],
            send_sem=swap_send.at[k], recv_sem=swap_recv.at[k],
            device_id=(peer(back), cell), device_id_type=MESH,
        ), peer(back)

    def forward(slot):
        @pl.when(has_next)
        def _():
            side_copy(0, slot).start()

        @pl.when(has_prev)
        def _():
            side_copy(1, slot).start()

    here_orbitals = orbitals[cell]
    next_orbitals = jnp.where(has_next, orbitals[jnp.minimum(cell + 1, cells - 1)], 0)
    row = lax.broadcasted_iota(jnp.int32, (width, width), 0)
    col = lax.broadcasted_iota(jnp.int32, (width, width), 1)
    loads[0].wait()
    loads[1].wait()
    vd = jnp.where((row < here_orbitals) & (col < here_orbitals), vdiag[...], 0.0)
    vu = jnp.where((row < here_orbitals) & (col < next_orbitals), vup[...], 0.0)
    vdiag[...] = vd
    vup[...] = vu
    for part in range(2):
        a, b, c = part * half // 2, (part + 1) * half // 2, half
        v_out[0, part] = pack(vu[a:b], vu[c + a:c + b], main)
        v_out[1, part] = pack(vd[a:b], vd[c + a:c + b], main)

    met = energies - 1 + jnp.where(has_next, 1, 0) + jnp.where(has_prev, 1, 0)
    pl.semaphore_wait(barrier, met)

    each_v(lambda copy: copy.start())

    loads[2].wait()
    loads[3].wait()
    scale = 1.0 / math.sqrt(energies)

    def polarize(step, carry):
        at = pl.ds(pl.multiple_of(step * 8, 8), 8)
        l_re = [less[0, m, at, :] for m in range(energies)]
        l_im = [less[1, m, at, :] for m in range(energies)]
        g_re = [greater[0, m, at, :] for m in range(energies)]
        g_im = [greater[1, m, at, :] for m in range(energies)]
        for shift in range(energies):
            real = imag = None
            for m in range(shift, energies):
                r = l_re[m] * g_re[m - shift] + l_im[m] * g_im[m - shift]
                i = l_im[m] * g_re[m - shift] - l_re[m] * g_im[m - shift]
                real = r if real is None else real + r
                imag = i if imag is None else imag + i
            shifted[shift, at, :] = pack(real * scale, imag * scale, main)
        return carry

    lax.fori_loop(0, rows // 8, polarize, 0)
    for k in range(1, energies):
        n = peer(k)
        outgoing[n] = shifted[offsets[n]]
        swap_copy(k).start()
    polar[me] = shifted[offsets[me]]
    forward(me)

    def cut(which, block):
        for e in range(energies):
            left[which, e] = left_operand(block[:, e * rows:(e + 1) * rows])

    vd = vdiag[...]
    cut(HERE, vd)
    if trading:
        for side, there in ((0, has_prev), (1, has_next)):
            @pl.when(there & (odd == side))
            def _():
                part = half_of(side)
                v_copy(side, part).wait_recv()
                trade_copy(side, part).start()

    def add_left(which, slot, block, first):
        product = dot(left[which, slot], left_rows(block))
        if first:
            a_sum[which] = product
        else:
            a_sum[which] += product

    def split(which):
        a = a_sum[which]
        edge = 2 * main + width - main
        return (
            right_operand(a[:, :main], a[:, 2 * main:edge]),
            right_operand(a[:, main:2 * main], a[:, edge:]),
        )

    def arrive(k):
        copy, slot = swap_arrival(k)
        copy.wait_recv()
        forward(slot)
        return slot

    slots = [me]

    def take_here(k):
        if k:
            slots.append(arrive(k))
        add_left(HERE, slots[k], polar[slots[k]], k == 0)

    def take_side(side, k):
        slot = slots[k]

        @pl.when(jnp.where(side == 0, has_prev, has_next))
        def _():
            side_copy(side, slot).wait_recv()

        add_left(2 - side, slot, beside[side, slot], k == 0)

    def take_right(which, first):
        for part, operand in enumerate(split(which)):
            product = dot(operand, right[which])
            if first:
                o_sum[part] = product
            else:
                o_sum[part] += product

    take_here(0)
    right[HERE] = right_rows(pack(vd.T, vup[...], main), main)
    vu = vup[...]
    cut(NEXT, vu)
    late, early = odd, 1 - odd
    last = energies - 1
    for k in range(1, last):
        take_here(k)

    for side, there in ((0, has_prev), (1, has_next)):
        for part in range(2):
            mine = (odd == side) & (half_of(side) == part) if trading else False

            @pl.when(there & jnp.logical_not(mine))
            def _():
                v_copy(side, part).wait_recv()

    def whole(side):
        parts = [unpack(v_in[side, part], main, width) for part in range(2)]
        return jnp.concatenate([p[0] for p in parts] + [p[1] for p in parts], axis=0)

    vp = whole(0)
    cut(PREV, vp.T)
    right[PREV] = right_rows(pack(vp, jnp.zeros_like(vp), main), main)
    vn = whole(1)
    right[NEXT] = right_rows(pack(vup[...].T, vn.T, main), main)

    for k in range(last):
        take_side(early, k)
        if k < last - 1:
            take_side(late, k)
    take_here(last)
    take_right(HERE, True)
    if last:
        take_side(late, last - 1)
    take_side(early, last)
    take_right(2 - early, False)
    take_side(late, last)
    for part, operand in enumerate(split(2 - late)):
        total = o_sum[part] + dot(operand, right[2 - late])
        diag[part], upper[part] = unpack(total, main, width)

    for k in range(1, energies):
        swap_copy(k).wait_send()
    each_v(lambda copy: copy.wait_send())
    if trading:
        for side, there in ((0, has_prev), (1, has_next)):
            @pl.when(there & (odd == side))
            def _():
                trade_copy(side, half_of(side)).wait_send()

    @pl.when(has_next)
    def _():
        for slot in range(energies):
            side_copy(0, slot).wait_send()

    @pl.when(has_prev)
    def _():
        for slot in range(energies):
            side_copy(1, slot).wait_send()


def solution(mesh):
    energies, cells = mesh.shape["energy"], mesh.shape["cell"]

    def per_device(green_less, green_greater, offsets, orbitals, coulomb_diag, coulomb_up):
        less = jnp.squeeze(green_less, 2)
        greater = jnp.squeeze(green_greater, 2)
        rows, width = less.shape[2], less.shape[3]
        main = width // 128 * 128
        depth = 3 * rows + -3 * rows % 128
        long = 3 * width + -3 * width % 128
        shape = jax.ShapeDtypeStruct((2, width, width), F32)
        anywhere = pl.BlockSpec(memory_space=pltpu.HBM)
        scalars = pl.BlockSpec(memory_space=pltpu.SMEM)
        dma = pltpu.SemaphoreType.DMA
        products = width * width * width * 2 * 8 * 3
        diag, upper = pl.pallas_call(
            functools.partial(kernel, energies, cells),
            out_shape=(shape, shape),
            in_specs=[scalars, scalars, anywhere, anywhere, anywhere, anywhere],
            out_specs=(pl.BlockSpec(memory_space=pltpu.VMEM),) * 2,
            scratch_shapes=[
                pltpu.VMEM(less.shape, F32),
                pltpu.VMEM(less.shape, F32),
                pltpu.VMEM((width, width), F32),
                pltpu.VMEM((width, width), F32),
                pltpu.VMEM((energies, rows, 2 * width), F32),
                pltpu.VMEM((energies, rows, 2 * width), F32),
                pltpu.VMEM((energies, rows, 2 * width), F32),
                pltpu.VMEM((2, energies, rows, 2 * width), F32),
                pltpu.VMEM((2, 2, width // 4, 2 * width), F32),
                pltpu.VMEM((2, 2, width // 4, 2 * width), F32),
                pltpu.VMEM((3, energies, width, depth), BF16),
                pltpu.VMEM((3, long, 2 * width), BF16),
                pltpu.VMEM((3, width, 2 * width), F32),
                pltpu.VMEM((2, width, 2 * width), F32),
                dma((4,)),
                dma((energies,)),
                dma((energies,)),
                dma((2, energies)),
                dma((2, energies)),
                dma((2, 2)),
                dma((2, 2)),
                dma,
            ],
            compiler_params=pltpu.CompilerParams(
                collective_id=0, has_side_effects=True, vmem_limit_bytes=62914560
            ),
            cost_estimate=pl.CostEstimate(
                flops=2 * products, bytes_accessed=4 * less.size * 4, transcendentals=0
            ),
            name="screen",
        )(offsets, orbitals, less, greater, coulomb_diag[0], coulomb_up[0])
        return diag[:, None, None], upper[:, None, None]

    in_specs = (
        P(None, None, "cell", "energy", None),
        P(None, None, "cell", "energy", None),
        P(),
        P(),
        P("cell", None, None),
        P("cell", None, None),
    )
    out_specs = (P(None, "energy", "cell", None, None), P(None, "energy", "cell", None, None))
    return jax.shard_map(
        per_device, mesh=mesh, in_specs=in_specs, out_specs=out_specs, check_vma=False
    )
```

```python
import functools
import math

import jax
import jax.numpy as jnp
from jax import lax
from jax.experimental import pallas as pl
from jax.experimental.pallas import tpu as pltpu
from jax.sharding import PartitionSpec as P

MESH = pl.DeviceIdType.MESH
F32 = jnp.float32
BF16 = jnp.bfloat16
HERE, NEXT, PREV = 0, 1, 2


def pack(first, second, main):
    return jnp.concatenate(
        [first[:, :main], second[:, :main], first[:, main:], second[:, main:]], axis=1
    )


def unpack(both, main, width):
    edge = 2 * main + width - main
    first = jnp.concatenate([both[:, :main], both[:, 2 * main:edge]], axis=1)
    second = jnp.concatenate([both[:, main:2 * main], both[:, edge:]], axis=1)
    return first, second


def halves(x):
    high = x.astype(BF16).astype(F32)
    return high, x - high


def lane_pad(parts):
    total = sum(p.shape[1] for p in parts)
    extra = -total % 128
    if extra:
        parts = parts + [jnp.zeros((parts[0].shape[0], extra), F32)]
    return jnp.concatenate(parts, axis=1).astype(BF16)


def row_pad(parts):
    total = sum(p.shape[0] for p in parts)
    extra = -total % 128
    if extra:
        parts = parts + [jnp.zeros((extra, parts[0].shape[1]), F32)]
    return jnp.concatenate(parts, axis=0).astype(BF16)


def left_operand(block):
    high, low = halves(block)
    return lane_pad([high, low, high])


def left_rows(rows):
    high, low = halves(rows)
    return row_pad([high, high, low])


def right_operand(main, tail):
    high, low = halves(main)
    end_high, end_low = halves(tail)
    return jnp.concatenate(
        [high.astype(BF16), low.astype(BF16), high.astype(BF16), lane_pad([end_high, end_low, end_high])],
        axis=1,
    )


def right_rows(block, main):
    high, low = halves(block)
    return row_pad(
        [high[:main], high[:main], low[:main], high[main:], high[main:], low[main:]]
    )


def dot(a, b):
    return jnp.dot(a, b, preferred_element_type=F32)


def kernel(
    energies, cells, offsets, orbitals, less_hbm, greater_hbm, vdiag_hbm, vup_hbm,
    diag_out, upper_out,
    less, greater, vdiag, vup, shifted, outgoing, polar, beside, v_out, v_in,
    left, right, a_sum, o_sum, diag, upper,
    in_sem, out_sem, swap_send, swap_recv, side_send, side_recv, v_send, v_recv,
):
    me = lax.axis_index("energy")
    cell = lax.axis_index("cell")
    rows, width = less.shape[2], less.shape[3]
    main = width // 128 * 128
    half = width // 2
    has_next = cell < cells - 1
    has_prev = cell > 0

    def peer(k):
        if energies & (energies - 1):
            return lax.rem(me + k, energies)
        other, bit = me, 1
        while bit <= k:
            if k & bit:
                other = other + bit * (1 - 2 * lax.rem(me // bit, 2))
            bit *= 2
        return other

    loads = [
        pltpu.make_async_copy(src, dst, in_sem.at[i])
        for i, (src, dst) in enumerate(
            [(vdiag_hbm, vdiag), (vup_hbm, vup), (less_hbm, less), (greater_hbm, greater)]
        )
    ]
    for load in loads:
        load.start()

    barrier = pltpu.get_barrier_semaphore()
    for k in range(1, energies):
        pl.semaphore_signal(barrier, inc=1, device_id=(peer(k), cell), device_id_type=MESH)

    @pl.when(has_next)
    def _():
        pl.semaphore_signal(barrier, inc=1, device_id=(me, cell + 1), device_id_type=MESH)

    @pl.when(has_prev)
    def _():
        pl.semaphore_signal(barrier, inc=1, device_id=(me, cell - 1), device_id_type=MESH)

    @pl.when(jnp.logical_not(has_prev))
    def _():
        beside[0] = jnp.zeros(beside.shape[1:], F32)
        v_in[0] = jnp.zeros(v_in.shape[1:], F32)

    @pl.when(jnp.logical_not(has_next))
    def _():
        beside[1] = jnp.zeros(beside.shape[1:], F32)
        v_in[1] = jnp.zeros(v_in.shape[1:], F32)

    late = lax.rem(cell, 2)
    early = 1 - late
    last = energies - 1

    def v_copy(side):
        return pltpu.make_async_remote_copy(
            src_ref=v_out.at[side], dst_ref=v_in.at[side],
            send_sem=v_send.at[side], recv_sem=v_recv.at[side],
            device_id=(me, cell + 1 - 2 * side), device_id_type=MESH,
        )

    cut_at = rows // 2 // 8 * 8

    def pieces(k):
        if k and k == last and cut_at:
            return [(0, pl.ds(0, cut_at)), (1, pl.ds(cut_at, rows - cut_at))]
        return [(0, pl.ds(0, rows))]

    def side_copy(side, k, piece, at):
        slot = slots[k]
        return pltpu.make_async_remote_copy(
            src_ref=polar.at[slot, at], dst_ref=beside.at[side, slot, at],
            send_sem=side_send.at[side, k, piece], recv_sem=side_recv.at[side, k, piece],
            device_id=(me, cell + 1 - 2 * side), device_id_type=MESH,
        )

    def side_copies(side, k):
        return [side_copy(side, k, piece, at) for piece, at in pieces(k)]

    def swap_copies(k):
        return [
            pltpu.make_async_remote_copy(
                src_ref=outgoing.at[peer(k), at], dst_ref=polar.at[me, at],
                send_sem=swap_send.at[k, piece], recv_sem=swap_recv.at[k, piece],
                device_id=(peer(k), cell), device_id_type=MESH,
            )
            for piece, at in pieces(k)
        ]

    def source(k):
        return peer(k if not energies & (energies - 1) else energies - k)

    slots = [me] + [source(k) for k in range(1, energies)]

    def swap_arrivals(k):
        return [
            pltpu.make_async_remote_copy(
                src_ref=outgoing.at[slots[k], at], dst_ref=polar.at[slots[k], at],
                send_sem=swap_send.at[k, piece], recv_sem=swap_recv.at[k, piece],
                device_id=(slots[k], cell), device_id_type=MESH,
            )
            for piece, at in pieces(k)
        ]

    def forward(k, piece, at):
        @pl.when(has_next)
        def _():
            side_copy(0, k, piece, at).start()

        @pl.when(has_prev)
        def _():
            side_copy(1, k, piece, at).start()

    here_orbitals = orbitals[cell]
    next_orbitals = jnp.where(has_next, orbitals[jnp.minimum(cell + 1, cells - 1)], 0)
    row = lax.broadcasted_iota(jnp.int32, (width, width), 0)
    col = lax.broadcasted_iota(jnp.int32, (width, width), 1)
    loads[0].wait()
    loads[1].wait()
    vd = jnp.where((row < here_orbitals) & (col < here_orbitals), vdiag[...], 0.0)
    vu = jnp.where((row < here_orbitals) & (col < next_orbitals), vup[...], 0.0)
    vdiag[...] = vd
    vup[...] = vu
    v_out[0] = pack(vu[:half], vu[half:], main)
    v_out[1] = pack(vd[:half], vd[half:], main)

    met = energies - 1 + jnp.where(has_next, 1, 0) + jnp.where(has_prev, 1, 0)
    pl.semaphore_wait(barrier, met)

    @pl.when(has_next)
    def _():
        v_copy(0).start()

    @pl.when(has_prev)
    def _():
        v_copy(1).start()

    loads[2].wait()
    loads[3].wait()
    scale = 1.0 / math.sqrt(energies)

    def polarize(step, carry):
        at = pl.ds(pl.multiple_of(step * 8, 8), 8)
        l_re = [less[0, m, at, :] for m in range(energies)]
        l_im = [less[1, m, at, :] for m in range(energies)]
        g_re = [greater[0, m, at, :] for m in range(energies)]
        g_im = [greater[1, m, at, :] for m in range(energies)]
        for shift in range(energies):
            real = imag = None
            for m in range(shift, energies):
                r = l_re[m] * g_re[m - shift] + l_im[m] * g_im[m - shift]
                i = l_im[m] * g_re[m - shift] - l_re[m] * g_im[m - shift]
                real = r if real is None else real + r
                imag = i if imag is None else imag + i
            shifted[shift, at, :] = pack(real * scale, imag * scale, main)
        return carry

    lax.fori_loop(0, rows // 8, polarize, 0)
    polar[me] = shifted[offsets[me]]
    forward(0, *pieces(0)[0])
    for k in range(1, energies):
        n = peer(k)
        outgoing[n] = shifted[offsets[n]]
        if k < last or last == 1:
            for copy in swap_copies(k):
                copy.start()

    def cut(which, block):
        for e in range(energies):
            left[which, e] = left_operand(block[:, e * rows:(e + 1) * rows])

    vd = vdiag[...]
    cut(HERE, vd)
    right[HERE] = right_rows(pack(vd.T, vup[...], main), main)
    cut(NEXT, vup[...])

    def add_left(which, slot, block, first):
        product = dot(left[which, slot], left_rows(block))
        if first:
            a_sum[which] = product
        else:
            a_sum[which] += product

    def split(which):
        a = a_sum[which]
        edge = 2 * main + width - main
        return (
            right_operand(a[:, :main], a[:, 2 * main:edge]),
            right_operand(a[:, main:2 * main], a[:, edge:]),
        )

    def arrive(k):
        for copy, (piece, at) in zip(swap_arrivals(k), pieces(k)):
            copy.wait_recv()
            forward(k, piece, at)

    def take_here(k):
        add_left(HERE, slots[k], polar[slots[k]], k == 0)

    def take_side(side, k):
        @pl.when(jnp.where(side == 0, has_prev, has_next))
        def _():
            for copy in side_copies(side, k):
                copy.wait_recv()

        add_left(2 - side, slots[k], beside[side, slots[k]], k == 0)

    def take_right(which, first):
        for part, operand in enumerate(split(which)):
            product = dot(operand, right[which])
            if first:
                o_sum[part] = product
            else:
                o_sum[part] += product

    take_here(0)
    for k in range(1, last):
        arrive(k)
    if last > 1:
        for k in range(1, last):
            for copy in swap_copies(k):
                copy.wait_send()
        for copy in swap_copies(last):
            copy.start()
    for k in range(1, last):
        take_here(k)

    @pl.when(has_prev)
    def _():
        v_copy(0).wait_recv()

    @pl.when(has_next)
    def _():
        v_copy(1).wait_recv()

    def whole(side):
        top, bottom = unpack(v_in[side], main, width)
        return jnp.concatenate([top, bottom], axis=0)

    vp = whole(0)
    cut(PREV, vp.T)
    right[PREV] = right_rows(pack(vp, jnp.zeros_like(vp), main), main)
    vn = whole(1)
    right[NEXT] = right_rows(pack(vup[...].T, vn.T, main), main)

    for k in range(last):
        take_side(early, k)
        if k < last - 1:
            take_side(late, k)
    if last:
        arrive(last)
        take_here(last)
    take_right(HERE, True)
    if last:
        take_side(late, last - 1)
    take_side(early, last)
    take_right(2 - early, False)
    take_side(late, last)
    writes = []
    for part, operand in enumerate(split(2 - late)):
        total = o_sum[part] + dot(operand, right[2 - late])
        diag[part], upper[part] = unpack(total, main, width)
        for i, (src, dst) in enumerate([(diag, diag_out), (upper, upper_out)]):
            writes.append(pltpu.make_async_copy(src.at[part], dst.at[part], out_sem.at[i, part]))
            writes[-1].start()

    for copy in swap_copies(last) if last else []:
        copy.wait_send()

    @pl.when(has_next)
    def _():
        v_copy(0).wait_send()
        for k in range(energies):
            for copy in side_copies(0, k):
                copy.wait_send()

    @pl.when(has_prev)
    def _():
        v_copy(1).wait_send()
        for k in range(energies):
            for copy in side_copies(1, k):
                copy.wait_send()

    for write in writes:
        write.wait()


def deliver(diag_in, upper_in, diag, upper, sem):
    rows = diag_in.shape[1]
    middle = rows // 16 * 8
    copies = []
    for i, (src, dst) in enumerate([(diag_in, diag), (upper_in, upper)]):
        for part in range(2):
            for j, at in enumerate([pl.ds(0, middle), pl.ds(middle, rows - middle)]):
                copies.append(pltpu.make_async_copy(src.at[part, at], dst.at[part, at], sem.at[i, part, j]))
    for copy in copies:
        copy.start()
    for copy in copies:
        copy.wait()


def solution(mesh):
    energies, cells = mesh.shape["energy"], mesh.shape["cell"]

    def per_device(green_less, green_greater, offsets, orbitals, coulomb_diag, coulomb_up):
        less = jnp.squeeze(green_less, 2)
        greater = jnp.squeeze(green_greater, 2)
        rows, width = less.shape[2], less.shape[3]
        main = width // 128 * 128
        depth = 3 * rows + -3 * rows % 128
        long = 3 * width + -3 * width % 128
        shape = jax.ShapeDtypeStruct((2, width, width), F32)
        anywhere = pl.BlockSpec(memory_space=pltpu.HBM)
        scalars = pl.BlockSpec(memory_space=pltpu.SMEM)
        dma = pltpu.SemaphoreType.DMA
        products = width * width * width * 2 * 8 * 3
        diag, upper = pl.pallas_call(
            functools.partial(kernel, energies, cells),
            out_shape=(shape, shape),
            in_specs=[scalars, scalars, anywhere, anywhere, anywhere, anywhere],
            out_specs=(anywhere, anywhere),
            scratch_shapes=[
                pltpu.VMEM(less.shape, F32),
                pltpu.VMEM(less.shape, F32),
                pltpu.VMEM((width, width), F32),
                pltpu.VMEM((width, width), F32),
                pltpu.VMEM((energies, rows, 2 * width), F32),
                pltpu.VMEM((energies, rows, 2 * width), F32),
                pltpu.VMEM((energies, rows, 2 * width), F32),
                pltpu.VMEM((2, energies, rows, 2 * width), F32),
                pltpu.VMEM((2, width // 2, 2 * width), F32),
                pltpu.VMEM((2, width // 2, 2 * width), F32),
                pltpu.VMEM((3, energies, width, depth), BF16),
                pltpu.VMEM((3, long, 2 * width), BF16),
                pltpu.VMEM((3, width, 2 * width), F32),
                pltpu.VMEM((2, width, 2 * width), F32),
                pltpu.VMEM((2, width, width), F32),
                pltpu.VMEM((2, width, width), F32),
                dma((4,)),
                dma((2, 2)),
                dma((energies, 2)),
                dma((energies, 2)),
                dma((2, energies, 2)),
                dma((2, energies, 2)),
                dma((2,)),
                dma((2,)),
            ],
            compiler_params=pltpu.CompilerParams(
                collective_id=0, has_side_effects=True, vmem_limit_bytes=62914560
            ),
            cost_estimate=pl.CostEstimate(
                flops=2 * products, bytes_accessed=4 * less.size * 4, transcendentals=0
            ),
            name="screen",
        )(offsets, orbitals, less, greater, coulomb_diag[0], coulomb_up[0])
        diag, upper = pl.pallas_call(
            deliver,
            out_shape=(shape, shape),
            in_specs=[pl.BlockSpec(memory_space=pl.ANY)] * 2,
            out_specs=(pl.BlockSpec(memory_space=pl.ANY),) * 2,
            scratch_shapes=[dma((2, 2, 2))],
            cost_estimate=pl.CostEstimate(
                flops=0, bytes_accessed=16 * width * width * 2, transcendentals=0
            ),
            compiler_params=pltpu.CompilerParams(vmem_limit_bytes=60 * 1024 * 1024),
            name="deliver",
        )(diag, upper)
        return diag[:, None, None], upper[:, None, None]

    in_specs = (
        P(None, None, "cell", "energy", None),
        P(None, None, "cell", "energy", None),
        P(),
        P(),
        P("cell", None, None),
        P("cell", None, None),
    )
    out_specs = (P(None, "energy", "cell", None, None), P(None, "energy", "cell", None, None))
    return jax.shard_map(
        per_device, mesh=mesh, in_specs=in_specs, out_specs=out_specs, check_vma=False
    )
```

```python
import functools
import math

import jax
import jax.numpy as jnp
from jax import lax
from jax.experimental import pallas as pl
from jax.experimental.pallas import tpu as pltpu
from jax.sharding import PartitionSpec as P

MESH = pl.DeviceIdType.MESH
F32 = jnp.float32
BF16 = jnp.bfloat16
HERE, NEXT, PREV = 0, 1, 2
SCREEN_BYTES = 60 * 1024 * 1024
DELIVER_BYTES = 60 * 1024 * 1024


def pack(first, second, main):
    return jnp.concatenate(
        [first[:, :main], second[:, :main], first[:, main:], second[:, main:]], axis=1
    )


def unpack(both, main, width):
    edge = 2 * main + width - main
    first = jnp.concatenate([both[:, :main], both[:, 2 * main:edge]], axis=1)
    second = jnp.concatenate([both[:, main:2 * main], both[:, edge:]], axis=1)
    return first, second


def halves(x):
    high = x.astype(BF16).astype(F32)
    return high, x - high


def lane_pad(parts):
    total = sum(p.shape[1] for p in parts)
    extra = -total % 128
    if extra:
        parts = parts + [jnp.zeros((parts[0].shape[0], extra), F32)]
    return jnp.concatenate(parts, axis=1).astype(BF16)


def row_pad(parts):
    total = sum(p.shape[0] for p in parts)
    extra = -total % 128
    if extra:
        parts = parts + [jnp.zeros((extra, parts[0].shape[1]), F32)]
    return jnp.concatenate(parts, axis=0).astype(BF16)


def left_operand(block):
    high, low = halves(block)
    return lane_pad([high, low, high])


def left_rows(rows):
    high, low = halves(rows)
    return row_pad([high, high, low])


def right_operand(main, tail):
    high, low = halves(main)
    end_high, end_low = halves(tail)
    return jnp.concatenate(
        [high.astype(BF16), low.astype(BF16), high.astype(BF16), lane_pad([end_high, end_low, end_high])],
        axis=1,
    )


def right_rows(block, main):
    high, low = halves(block)
    return row_pad(
        [high[:main], high[:main], low[:main], high[main:], high[main:], low[main:]]
    )


def dot(a, b):
    return jnp.dot(a, b, preferred_element_type=F32)


def kernel(
    energies, cells, offsets, orbitals, less_hbm, greater_hbm, vdiag_hbm, vup_hbm,
    diag_out, upper_out,
    less, greater, vdiag, vup, shifted, outgoing, polar, beside, v_out, v_in,
    left, right, stack, o_sum, diag, upper,
    in_sem, out_sem, swap_send, swap_recv, side_send, side_recv, v_send, v_recv,
):
    me = lax.axis_index("energy")
    cell = lax.axis_index("cell")
    rows, width = less.shape[2], less.shape[3]
    main = width // 128 * 128
    half = width // 2
    has_next = cell < cells - 1
    has_prev = cell > 0

    def peer(k):
        if energies & (energies - 1):
            return lax.rem(me + k, energies)
        other, bit = me, 1
        while bit <= k:
            if k & bit:
                other = other + bit * (1 - 2 * lax.rem(me // bit, 2))
            bit *= 2
        return other

    def load(number, src, dst):
        pieces_of = []
        middle = src.shape[0] // 2
        for i, at in enumerate([pl.ds(0, middle), pl.ds(middle, src.shape[0] - middle)]):
            pieces_of.append(pltpu.make_async_copy(src.at[at], dst.at[at], in_sem.at[number, i]))
            pieces_of[-1].start()
        return pieces_of

    v_loads = load(0, vdiag_hbm, vdiag) + load(1, vup_hbm, vup)
    loads = load(2, less_hbm, less) + load(3, greater_hbm, greater)

    barrier = pltpu.get_barrier_semaphore()
    for k in range(1, energies):
        pl.semaphore_signal(barrier, inc=1, device_id=(peer(k), cell), device_id_type=MESH)

    @pl.when(has_next)
    def _():
        pl.semaphore_signal(barrier, inc=1, device_id=(me, cell + 1), device_id_type=MESH)

    @pl.when(has_prev)
    def _():
        pl.semaphore_signal(barrier, inc=1, device_id=(me, cell - 1), device_id_type=MESH)

    @pl.when(jnp.logical_not(has_prev))
    def _():
        beside[0] = jnp.zeros(beside.shape[1:], F32)
        v_in[0] = jnp.zeros(v_in.shape[1:], F32)

    @pl.when(jnp.logical_not(has_next))
    def _():
        beside[1] = jnp.zeros(beside.shape[1:], F32)
        v_in[1] = jnp.zeros(v_in.shape[1:], F32)

    late = lax.rem(cell, 2)
    early = 1 - late
    last = energies - 1

    def v_copy(side):
        return pltpu.make_async_remote_copy(
            src_ref=v_out.at[side], dst_ref=v_in.at[side],
            send_sem=v_send.at[side], recv_sem=v_recv.at[side],
            device_id=(me, cell + 1 - 2 * side), device_id_type=MESH,
        )

    cut_at = rows // 2 // 8 * 8

    def pieces(k):
        if k and k == last and cut_at:
            return [(0, pl.ds(0, cut_at)), (1, pl.ds(cut_at, rows - cut_at))]
        return [(0, pl.ds(0, rows))]

    def side_copy(side, k, piece, at):
        slot = slots[k]
        return pltpu.make_async_remote_copy(
            src_ref=polar.at[slot, at], dst_ref=beside.at[side, slot, at],
            send_sem=side_send.at[side, k, piece], recv_sem=side_recv.at[side, k, piece],
            device_id=(me, cell + 1 - 2 * side), device_id_type=MESH,
        )

    def side_copies(side, k):
        return [side_copy(side, k, piece, at) for piece, at in pieces(k)]

    def swap_copies(k):
        return [
            pltpu.make_async_remote_copy(
                src_ref=outgoing.at[peer(k), at], dst_ref=polar.at[me, at],
                send_sem=swap_send.at[k, piece], recv_sem=swap_recv.at[k, piece],
                device_id=(peer(k), cell), device_id_type=MESH,
            )
            for piece, at in pieces(k)
        ]

    def source(k):
        return peer(k if not energies & (energies - 1) else energies - k)

    slots = [me] + [source(k) for k in range(1, energies)]

    def swap_arrivals(k):
        return [
            pltpu.make_async_remote_copy(
                src_ref=outgoing.at[slots[k], at], dst_ref=polar.at[slots[k], at],
                send_sem=swap_send.at[k, piece], recv_sem=swap_recv.at[k, piece],
                device_id=(slots[k], cell), device_id_type=MESH,
            )
            for piece, at in pieces(k)
        ]

    def forward(k, piece, at):
        @pl.when(has_next)
        def _():
            side_copy(0, k, piece, at).start()

        @pl.when(has_prev)
        def _():
            side_copy(1, k, piece, at).start()

    here_orbitals = orbitals[cell]
    next_orbitals = jnp.where(has_next, orbitals[jnp.minimum(cell + 1, cells - 1)], 0)
    row = lax.broadcasted_iota(jnp.int32, (width, width), 0)
    col = lax.broadcasted_iota(jnp.int32, (width, width), 1)
    for copy in v_loads:
        copy.wait()
    vd = jnp.where((row < here_orbitals) & (col < here_orbitals), vdiag[...], 0.0)
    vu = jnp.where((row < here_orbitals) & (col < next_orbitals), vup[...], 0.0)
    vdiag[...] = vd
    vup[...] = vu
    v_out[0] = pack(vu[:half], vu[half:], main)
    v_out[1] = pack(vd[:half], vd[half:], main)

    met = energies - 1 + jnp.where(has_next, 1, 0) + jnp.where(has_prev, 1, 0)
    pl.semaphore_wait(barrier, met)

    @pl.when(has_next)
    def _():
        v_copy(0).start()

    @pl.when(has_prev)
    def _():
        v_copy(1).start()

    for copy in loads:
        copy.wait()
    scale = 1.0 / math.sqrt(energies)

    def polarize(step, carry):
        at = pl.ds(pl.multiple_of(step * 8, 8), 8)
        l_re = [less[0, m, at, :] for m in range(energies)]
        l_im = [less[1, m, at, :] for m in range(energies)]
        g_re = [greater[0, m, at, :] for m in range(energies)]
        g_im = [greater[1, m, at, :] for m in range(energies)]
        for shift in range(energies):
            real = imag = None
            for m in range(shift, energies):
                r = l_re[m] * g_re[m - shift] + l_im[m] * g_im[m - shift]
                i = l_im[m] * g_re[m - shift] - l_re[m] * g_im[m - shift]
                real = r if real is None else real + r
                imag = i if imag is None else imag + i
            shifted[shift, at, :] = pack(real * scale, imag * scale, main)
        return carry

    lax.fori_loop(0, rows // 8, polarize, 0)
    polar[me] = shifted[offsets[me]]
    forward(0, *pieces(0)[0])
    for k in range(1, energies):
        n = peer(k)
        outgoing[n] = shifted[offsets[n]]
        if k < last or last == 1:
            for copy in swap_copies(k):
                copy.start()

    def cut(which, block):
        for e in range(energies):
            left[which, e] = left_operand(block[:, e * rows:(e + 1) * rows])

    vd = vdiag[...]
    cut(HERE, vd)
    right[HERE] = right_rows(pack(vd.T, vup[...], main), main)
    cut(NEXT, vup[...])

    def stacked(block):
        edge = 2 * main + width - main
        return right_operand(
            jnp.concatenate([block[:, :main], block[:, main:2 * main]], axis=0),
            jnp.concatenate([block[:, 2 * main:edge], block[:, edge:]], axis=0),
        )

    def add_left(which, block_of):
        operand = jnp.concatenate([left[which, slots[k]] for k in range(last)], axis=1)
        facing = jnp.concatenate([left_rows(block_of(slots[k])) for k in range(last)], axis=0)
        stack[which] = stacked(dot(operand, facing))

    def arrive(k):
        for copy, (piece, at) in zip(swap_arrivals(k), pieces(k)):
            copy.wait_recv()
            forward(k, piece, at)

    def wait_side(side, k):
        @pl.when(jnp.where(side == 0, has_prev, has_next))
        def _():
            for copy in side_copies(side, k):
                copy.wait_recv()

    def take_side(side):
        for k in range(last):
            wait_side(side, k)
        add_left(2 - side, lambda slot: beside[side, slot])

    for k in range(1, last):
        arrive(k)
    if last > 1:
        for k in range(1, last):
            for copy in swap_copies(k):
                copy.wait_send()
        for copy in swap_copies(last):
            copy.start()
    add_left(HERE, lambda slot: polar[slot])

    @pl.when(has_prev)
    def _():
        v_copy(0).wait_recv()

    @pl.when(has_next)
    def _():
        v_copy(1).wait_recv()

    def whole(side):
        top, bottom = unpack(v_in[side], main, width)
        return jnp.concatenate([top, bottom], axis=0)

    vp = whole(0)
    cut(PREV, vp.T)
    right[PREV] = right_rows(pack(vp, jnp.zeros_like(vp), main), main)
    vn = whole(1)
    right[NEXT] = right_rows(pack(vup[...].T, vn.T, main), main)

    take_side(early)
    arrive(last)
    take_side(late)
    kinds = (HERE, NEXT, PREV)
    o_sum[...] = dot(
        jnp.concatenate([stack[which] for which in kinds], axis=1),
        jnp.concatenate([right[which] for which in kinds], axis=0),
    )
    wait_side(early, last)
    wait_side(late, last)

    slot = slots[last]
    ends = [polar[slot], beside[1, slot], beside[0, slot]]
    turned = [dot(stacked(end), right[which]) for which, end in zip(kinds, ends)]
    operand = jnp.concatenate([left[which, slot] for which in kinds], axis=1)
    writes = []
    for part in range(2):
        facing = [left_rows(t[part * rows:(part + 1) * rows]) for t in turned]
        total = o_sum[part * width:(part + 1) * width, :] + dot(operand, jnp.concatenate(facing, axis=0))
        diag[part], upper[part] = unpack(total, main, width)
        for i, (src, dst) in enumerate([(diag, diag_out), (upper, upper_out)]):
            writes.append(pltpu.make_async_copy(src.at[part], dst.at[part], out_sem.at[i, part]))
            writes[-1].start()

    for copy in swap_copies(last):
        copy.wait_send()

    @pl.when(has_next)
    def _():
        v_copy(0).wait_send()
        for k in range(energies):
            for copy in side_copies(0, k):
                copy.wait_send()

    @pl.when(has_prev)
    def _():
        v_copy(1).wait_send()
        for k in range(energies):
            for copy in side_copies(1, k):
                copy.wait_send()

    for write in writes:
        write.wait()


def deliver(diag_in, upper_in, diag, upper, held, in_sem, out_sem):
    rows = diag_in.shape[1]
    middle = rows // 16 * 8
    copies = []
    for i, (src, dst) in enumerate([(diag_in, diag), (upper_in, upper)]):
        for part in range(2):
            for j, at in enumerate([pl.ds(0, middle), pl.ds(middle, rows - middle)]):
                here = held.at[i, part, at]
                copies.append((
                    pltpu.make_async_copy(src.at[part, at], here, in_sem.at[i, part, j]),
                    pltpu.make_async_copy(here, dst.at[part, at], out_sem.at[i, part, j]),
                ))
    for arriving, _ in copies:
        arriving.start()
    for arriving, leaving in copies:
        arriving.wait()
        leaving.start()
    for _, leaving in copies:
        leaving.wait()


def solution(mesh):
    energies, cells = mesh.shape["energy"], mesh.shape["cell"]

    def per_device(green_less, green_greater, offsets, orbitals, coulomb_diag, coulomb_up):
        less = jnp.squeeze(green_less, 2)
        greater = jnp.squeeze(green_greater, 2)
        rows, width = less.shape[2], less.shape[3]
        main = width // 128 * 128
        depth = 3 * rows + -3 * rows % 128
        long = 3 * width + -3 * width % 128
        shape = jax.ShapeDtypeStruct((2, width, width), F32)
        anywhere = pl.BlockSpec(memory_space=pltpu.HBM)
        scalars = pl.BlockSpec(memory_space=pltpu.SMEM)
        dma = pltpu.SemaphoreType.DMA
        products = width * width * width * 2 * 8 * 3
        diag, upper = pl.pallas_call(
            functools.partial(kernel, energies, cells),
            out_shape=(shape, shape),
            in_specs=[scalars, scalars, anywhere, anywhere, anywhere, anywhere],
            out_specs=(anywhere, anywhere),
            scratch_shapes=[
                pltpu.VMEM(less.shape, F32),
                pltpu.VMEM(less.shape, F32),
                pltpu.VMEM((width, width), F32),
                pltpu.VMEM((width, width), F32),
                pltpu.VMEM((energies, rows, 2 * width), F32),
                pltpu.VMEM((energies, rows, 2 * width), F32),
                pltpu.VMEM((energies, rows, 2 * width), F32),
                pltpu.VMEM((2, energies, rows, 2 * width), F32),
                pltpu.VMEM((2, width // 2, 2 * width), F32),
                pltpu.VMEM((2, width // 2, 2 * width), F32),
                pltpu.VMEM((3, energies, width, depth), BF16),
                pltpu.VMEM((3, long, 2 * width), BF16),
                pltpu.VMEM((3, 2 * width, long), BF16),
                pltpu.VMEM((2 * width, 2 * width), F32),
                pltpu.VMEM((2, width, width), F32),
                pltpu.VMEM((2, width, width), F32),
                dma((4, 2)),
                dma((2, 2)),
                dma((energies, 2)),
                dma((energies, 2)),
                dma((2, energies, 2)),
                dma((2, energies, 2)),
                dma((2,)),
                dma((2,)),
            ],
            compiler_params=pltpu.CompilerParams(
                collective_id=0, has_side_effects=True, vmem_limit_bytes=SCREEN_BYTES
            ),
            cost_estimate=pl.CostEstimate(
                flops=2 * products, bytes_accessed=4 * less.size * 4, transcendentals=0
            ),
            name="screen",
        )(offsets, orbitals, less, greater, coulomb_diag[0], coulomb_up[0])
        diag, upper = pl.pallas_call(
            deliver,
            out_shape=(shape, shape),
            in_specs=[pl.BlockSpec(memory_space=pl.ANY)] * 2,
            out_specs=(pl.BlockSpec(memory_space=pl.ANY),) * 2,
            scratch_shapes=[pltpu.VMEM((2,) + shape.shape, F32), dma((2, 2, 2)), dma((2, 2, 2))],
            cost_estimate=pl.CostEstimate(
                flops=0, bytes_accessed=16 * width * width * 2, transcendentals=0
            ),
            compiler_params=pltpu.CompilerParams(vmem_limit_bytes=DELIVER_BYTES),
            name="deliver",
        )(diag, upper)
        return diag[:, None, None], upper[:, None, None]

    in_specs = (
        P(None, None, "cell", "energy", None),
        P(None, None, "cell", "energy", None),
        P(),
        P(),
        P("cell", None, None),
        P("cell", None, None),
    )
    out_specs = (P(None, "energy", "cell", None, None), P(None, "energy", "cell", None, None))
    return jax.shard_map(
        per_device, mesh=mesh, in_specs=in_specs, out_specs=out_specs, check_vma=False
    )
```

```python
import functools
import math

import jax
import jax.numpy as jnp
from jax import lax
from jax.experimental import pallas as pl
from jax.experimental.pallas import tpu as pltpu
from jax.sharding import PartitionSpec as P

MESH = pl.DeviceIdType.MESH
F32 = jnp.float32
BF16 = jnp.bfloat16
HERE, NEXT, PREV = 0, 1, 2
SCREEN_BYTES = 60 * 1024 * 1024
DELIVER_BYTES = 60 * 1024 * 1024


def pack(first, second, main):
    return jnp.concatenate(
        [first[:, :main], second[:, :main], first[:, main:], second[:, main:]], axis=1
    )


def unpack(both, main, width):
    edge = 2 * main + width - main
    first = jnp.concatenate([both[:, :main], both[:, 2 * main:edge]], axis=1)
    second = jnp.concatenate([both[:, main:2 * main], both[:, edge:]], axis=1)
    return first, second


def halves(x):
    high = x.astype(BF16).astype(F32)
    return high, x - high


def lane_pad(parts):
    total = sum(p.shape[1] for p in parts)
    extra = -total % 128
    if extra:
        parts = parts + [jnp.zeros((parts[0].shape[0], extra), F32)]
    return jnp.concatenate(parts, axis=1).astype(BF16)


def row_pad(parts):
    total = sum(p.shape[0] for p in parts)
    extra = -total % 128
    if extra:
        parts = parts + [jnp.zeros((extra, parts[0].shape[1]), F32)]
    return jnp.concatenate(parts, axis=0).astype(BF16)


def left_operand(block):
    high, low = halves(block)
    return lane_pad([high, low, high])


def left_rows(rows):
    high, low = halves(rows)
    return row_pad([high, high, low])


def right_operand(main, tail):
    high, low = halves(main)
    end_high, end_low = halves(tail)
    return jnp.concatenate(
        [high.astype(BF16), low.astype(BF16), high.astype(BF16), lane_pad([end_high, end_low, end_high])],
        axis=1,
    )


def right_rows(block, main):
    high, low = halves(block)
    return row_pad(
        [high[:main], high[:main], low[:main], high[main:], high[main:], low[main:]]
    )


def dot(a, b):
    return jnp.dot(a, b, preferred_element_type=F32)


def kernel(
    energies, cells, offsets, orbitals, less_hbm, greater_hbm, vdiag_hbm, vup_hbm,
    diag_out, upper_out,
    less, greater, vdiag, vup, shifted, outgoing, polar, beside, v_out, v_in,
    left, right, a_sum, o_sum, diag, upper,
    in_sem, out_sem, swap_send, swap_recv, side_send, side_recv, v_send, v_recv,
):
    me = lax.axis_index("energy")
    cell = lax.axis_index("cell")
    rows, width = less.shape[2], less.shape[3]
    main = width // 128 * 128
    half = width // 2
    has_next = cell < cells - 1
    has_prev = cell > 0

    def peer(k):
        if energies & (energies - 1):
            return lax.rem(me + k, energies)
        other, bit = me, 1
        while bit <= k:
            if k & bit:
                other = other + bit * (1 - 2 * lax.rem(me // bit, 2))
            bit *= 2
        return other

    def load(number, src, dst):
        pieces_of = []
        middle = src.shape[0] // 2
        for i, at in enumerate([pl.ds(0, middle), pl.ds(middle, src.shape[0] - middle)]):
            pieces_of.append(pltpu.make_async_copy(src.at[at], dst.at[at], in_sem.at[number, i]))
            pieces_of[-1].start()
        return pieces_of

    v_loads = load(0, vdiag_hbm, vdiag) + load(1, vup_hbm, vup)
    loads = load(2, less_hbm, less) + load(3, greater_hbm, greater)

    barrier = pltpu.get_barrier_semaphore()
    for k in range(1, energies):
        pl.semaphore_signal(barrier, inc=1, device_id=(peer(k), cell), device_id_type=MESH)

    @pl.when(has_next)
    def _():
        pl.semaphore_signal(barrier, inc=1, device_id=(me, cell + 1), device_id_type=MESH)

    @pl.when(has_prev)
    def _():
        pl.semaphore_signal(barrier, inc=1, device_id=(me, cell - 1), device_id_type=MESH)

    @pl.when(jnp.logical_not(has_prev))
    def _():
        beside[0] = jnp.zeros(beside.shape[1:], F32)
        v_in[0] = jnp.zeros(v_in.shape[1:], F32)

    @pl.when(jnp.logical_not(has_next))
    def _():
        beside[1] = jnp.zeros(beside.shape[1:], F32)
        v_in[1] = jnp.zeros(v_in.shape[1:], F32)

    late = lax.rem(cell, 2)
    early = 1 - late
    last = energies - 1

    def v_copy(side):
        return pltpu.make_async_remote_copy(
            src_ref=v_out.at[side], dst_ref=v_in.at[side],
            send_sem=v_send.at[side], recv_sem=v_recv.at[side],
            device_id=(me, cell + 1 - 2 * side), device_id_type=MESH,
        )

    cut_at = rows // 2 // 8 * 8

    def pieces(k):
        if k and k == last and cut_at:
            return [(0, pl.ds(0, cut_at)), (1, pl.ds(cut_at, rows - cut_at))]
        return [(0, pl.ds(0, rows))]

    def side_copy(side, k, piece, at):
        slot = slots[k]
        return pltpu.make_async_remote_copy(
            src_ref=polar.at[slot, at], dst_ref=beside.at[side, slot, at],
            send_sem=side_send.at[side, k, piece], recv_sem=side_recv.at[side, k, piece],
            device_id=(me, cell + 1 - 2 * side), device_id_type=MESH,
        )

    def side_copies(side, k):
        return [side_copy(side, k, piece, at) for piece, at in pieces(k)]

    def swap_copies(k):
        return [
            pltpu.make_async_remote_copy(
                src_ref=outgoing.at[peer(k), at], dst_ref=polar.at[me, at],
                send_sem=swap_send.at[k, piece], recv_sem=swap_recv.at[k, piece],
                device_id=(peer(k), cell), device_id_type=MESH,
            )
            for piece, at in pieces(k)
        ]

    def source(k):
        return peer(k if not energies & (energies - 1) else energies - k)

    slots = [me] + [source(k) for k in range(1, energies)]

    def swap_arrivals(k):
        return [
            pltpu.make_async_remote_copy(
                src_ref=outgoing.at[slots[k], at], dst_ref=polar.at[slots[k], at],
                send_sem=swap_send.at[k, piece], recv_sem=swap_recv.at[k, piece],
                device_id=(slots[k], cell), device_id_type=MESH,
            )
            for piece, at in pieces(k)
        ]

    def forward(k, piece, at):
        @pl.when(has_next)
        def _():
            side_copy(0, k, piece, at).start()

        @pl.when(has_prev)
        def _():
            side_copy(1, k, piece, at).start()

    here_orbitals = orbitals[cell]
    next_orbitals = jnp.where(has_next, orbitals[jnp.minimum(cell + 1, cells - 1)], 0)
    row = lax.broadcasted_iota(jnp.int32, (width, width), 0)
    col = lax.broadcasted_iota(jnp.int32, (width, width), 1)
    for copy in v_loads:
        copy.wait()
    vd = jnp.where((row < here_orbitals) & (col < here_orbitals), vdiag[...], 0.0)
    vu = jnp.where((row < here_orbitals) & (col < next_orbitals), vup[...], 0.0)
    vdiag[...] = vd
    vup[...] = vu
    v_out[0] = pack(vu[:half], vu[half:], main)
    v_out[1] = pack(vd[:half], vd[half:], main)

    met = energies - 1 + jnp.where(has_next, 1, 0) + jnp.where(has_prev, 1, 0)
    pl.semaphore_wait(barrier, met)

    @pl.when(has_next)
    def _():
        v_copy(0).start()

    @pl.when(has_prev)
    def _():
        v_copy(1).start()

    for copy in loads:
        copy.wait()
    scale = 1.0 / math.sqrt(energies)

    def polarize(step, carry):
        at = pl.ds(pl.multiple_of(step * 8, 8), 8)
        l_re = [less[0, m, at, :] for m in range(energies)]
        l_im = [less[1, m, at, :] for m in range(energies)]
        g_re = [greater[0, m, at, :] for m in range(energies)]
        g_im = [greater[1, m, at, :] for m in range(energies)]
        for shift in range(energies):
            real = imag = None
            for m in range(shift, energies):
                r = l_re[m] * g_re[m - shift] + l_im[m] * g_im[m - shift]
                i = l_im[m] * g_re[m - shift] - l_re[m] * g_im[m - shift]
                real = r if real is None else real + r
                imag = i if imag is None else imag + i
            shifted[shift, at, :] = pack(real * scale, imag * scale, main)
        return carry

    lax.fori_loop(0, rows // 8, polarize, 0)
    polar[me] = shifted[offsets[me]]
    forward(0, *pieces(0)[0])
    for k in range(1, energies):
        n = peer(k)
        outgoing[n] = shifted[offsets[n]]
        if k < last or last == 1:
            for copy in swap_copies(k):
                copy.start()

    def cut(which, block):
        for e in range(energies):
            left[which, e] = left_operand(block[:, e * rows:(e + 1) * rows])

    vd = vdiag[...]
    cut(HERE, vd)
    right[HERE] = right_rows(pack(vd.T, vup[...], main), main)
    cut(NEXT, vup[...])

    def stacked(block):
        edge = 2 * main + width - main
        return right_operand(
            jnp.concatenate([block[:, :main], block[:, main:2 * main]], axis=0),
            jnp.concatenate([block[:, 2 * main:edge], block[:, edge:]], axis=0),
        )

    def add_left(which, slot, block, first):
        product = dot(left[which, slot], left_rows(block))
        if first:
            a_sum[which] = product
        else:
            a_sum[which] += product

    def arrive(k):
        for copy, (piece, at) in zip(swap_arrivals(k), pieces(k)):
            copy.wait_recv()
            forward(k, piece, at)

    def take_here(k):
        add_left(HERE, slots[k], polar[slots[k]], k == 0)

    def wait_side(side, k):
        @pl.when(jnp.where(side == 0, has_prev, has_next))
        def _():
            for copy in side_copies(side, k):
                copy.wait_recv()

    def take_side(side, k):
        wait_side(side, k)
        add_left(2 - side, slots[k], beside[side, slots[k]], k == 0)

    def take_right(which, first):
        product = dot(stacked(a_sum[which]), right[which])
        if first:
            o_sum[...] = product
        else:
            o_sum[...] += product

    take_here(0)
    for k in range(1, last):
        arrive(k)
    if last > 1:
        for k in range(1, last):
            for copy in swap_copies(k):
                copy.wait_send()
        for copy in swap_copies(last):
            copy.start()
    for k in range(1, last):
        take_here(k)

    @pl.when(has_prev)
    def _():
        v_copy(0).wait_recv()

    @pl.when(has_next)
    def _():
        v_copy(1).wait_recv()

    def whole(side):
        top, bottom = unpack(v_in[side], main, width)
        return jnp.concatenate([top, bottom], axis=0)

    vp = whole(0)
    cut(PREV, vp.T)
    right[PREV] = right_rows(pack(vp, jnp.zeros_like(vp), main), main)
    vn = whole(1)
    right[NEXT] = right_rows(pack(vup[...].T, vn.T, main), main)

    for k in range(last):
        take_side(early, k)
        if k < last - 1:
            take_side(late, k)
    arrive(last)
    take_here(last)
    take_right(HERE, True)
    take_side(late, last - 1)
    take_side(early, last)
    take_right(2 - early, False)
    take_right(2 - late, False)

    wait_side(late, last)
    slot = slots[last]
    turned = dot(stacked(beside[late, slot]), right[2 - late])
    writes = []
    for part in range(2):
        facing = left_rows(turned[part * rows:(part + 1) * rows])
        total = o_sum[part * width:(part + 1) * width, :] + dot(left[2 - late, slot], facing)
        diag[part], upper[part] = unpack(total, main, width)
        for i, (src, dst) in enumerate([(diag, diag_out), (upper, upper_out)]):
            writes.append(pltpu.make_async_copy(src.at[part], dst.at[part], out_sem.at[i, part]))
            writes[-1].start()

    for copy in swap_copies(last):
        copy.wait_send()

    @pl.when(has_next)
    def _():
        v_copy(0).wait_send()
        for k in range(energies):
            for copy in side_copies(0, k):
                copy.wait_send()

    @pl.when(has_prev)
    def _():
        v_copy(1).wait_send()
        for k in range(energies):
            for copy in side_copies(1, k):
                copy.wait_send()

    for write in writes:
        write.wait()


def deliver(diag_in, upper_in, diag, upper, held, in_sem, out_sem):
    rows = diag_in.shape[1]
    middle = rows // 16 * 8
    copies = []
    for i, (src, dst) in enumerate([(diag_in, diag), (upper_in, upper)]):
        for part in range(2):
            for j, at in enumerate([pl.ds(0, middle), pl.ds(middle, rows - middle)]):
                here = held.at[i, part, at]
                copies.append((
                    pltpu.make_async_copy(src.at[part, at], here, in_sem.at[i, part, j]),
                    pltpu.make_async_copy(here, dst.at[part, at], out_sem.at[i, part, j]),
                ))
    for arriving, _ in copies:
        arriving.start()
    for arriving, leaving in copies:
        arriving.wait()
        leaving.start()
    for _, leaving in copies:
        leaving.wait()


def solution(mesh):
    energies, cells = mesh.shape["energy"], mesh.shape["cell"]

    def per_device(green_less, green_greater, offsets, orbitals, coulomb_diag, coulomb_up):
        less = jnp.squeeze(green_less, 2)
        greater = jnp.squeeze(green_greater, 2)
        rows, width = less.shape[2], less.shape[3]
        main = width // 128 * 128
        depth = 3 * rows + -3 * rows % 128
        long = 3 * width + -3 * width % 128
        shape = jax.ShapeDtypeStruct((2, width, width), F32)
        anywhere = pl.BlockSpec(memory_space=pltpu.HBM)
        scalars = pl.BlockSpec(memory_space=pltpu.SMEM)
        dma = pltpu.SemaphoreType.DMA
        products = width * width * width * 2 * 8 * 3
        diag, upper = pl.pallas_call(
            functools.partial(kernel, energies, cells),
            out_shape=(shape, shape),
            in_specs=[scalars, scalars, anywhere, anywhere, anywhere, anywhere],
            out_specs=(anywhere, anywhere),
            scratch_shapes=[
                pltpu.VMEM(less.shape, F32),
                pltpu.VMEM(less.shape, F32),
                pltpu.VMEM((width, width), F32),
                pltpu.VMEM((width, width), F32),
                pltpu.VMEM((energies, rows, 2 * width), F32),
                pltpu.VMEM((energies, rows, 2 * width), F32),
                pltpu.VMEM((energies, rows, 2 * width), F32),
                pltpu.VMEM((2, energies, rows, 2 * width), F32),
                pltpu.VMEM((2, width // 2, 2 * width), F32),
                pltpu.VMEM((2, width // 2, 2 * width), F32),
                pltpu.VMEM((3, energies, width, depth), BF16),
                pltpu.VMEM((3, long, 2 * width), BF16),
                pltpu.VMEM((3, width, 2 * width), F32),
                pltpu.VMEM((2 * width, 2 * width), F32),
                pltpu.VMEM((2, width, width), F32),
                pltpu.VMEM((2, width, width), F32),
                dma((4, 2)),
                dma((2, 2)),
                dma((energies, 2)),
                dma((energies, 2)),
                dma((2, energies, 2)),
                dma((2, energies, 2)),
                dma((2,)),
                dma((2,)),
            ],
            compiler_params=pltpu.CompilerParams(
                collective_id=0, has_side_effects=True, vmem_limit_bytes=SCREEN_BYTES
            ),
            cost_estimate=pl.CostEstimate(
                flops=2 * products, bytes_accessed=4 * less.size * 4, transcendentals=0
            ),
            name="screen",
        )(offsets, orbitals, less, greater, coulomb_diag[0], coulomb_up[0])
        diag, upper = pl.pallas_call(
            deliver,
            out_shape=(shape, shape),
            in_specs=[pl.BlockSpec(memory_space=pl.ANY)] * 2,
            out_specs=(pl.BlockSpec(memory_space=pl.ANY),) * 2,
            scratch_shapes=[pltpu.VMEM((2,) + shape.shape, F32), dma((2, 2, 2)), dma((2, 2, 2))],
            cost_estimate=pl.CostEstimate(
                flops=0, bytes_accessed=16 * width * width * 2, transcendentals=0
            ),
            compiler_params=pltpu.CompilerParams(vmem_limit_bytes=DELIVER_BYTES),
            name="deliver",
        )(diag, upper)
        return diag[:, None, None], upper[:, None, None]

    in_specs = (
        P(None, None, "cell", "energy", None),
        P(None, None, "cell", "energy", None),
        P(),
        P(),
        P("cell", None, None),
        P("cell", None, None),
    )
    out_specs = (P(None, "energy", "cell", None, None), P(None, "energy", "cell", None, None))
    return jax.shard_map(
        per_device, mesh=mesh, in_specs=in_specs, out_specs=out_specs, check_vma=False
    )
```

```python
import functools
import math

import jax
import jax.numpy as jnp
from jax import lax
from jax.experimental import pallas as pl
from jax.experimental.pallas import tpu as pltpu
from jax.sharding import PartitionSpec as P

MESH = pl.DeviceIdType.MESH
F32 = jnp.float32
BF16 = jnp.bfloat16
HERE, NEXT, PREV = 0, 1, 2


def pack(first, second, main):
    return jnp.concatenate(
        [first[:, :main], second[:, :main], first[:, main:], second[:, main:]], axis=1
    )


def unpack(both, main, width):
    edge = 2 * main + width - main
    first = jnp.concatenate([both[:, :main], both[:, 2 * main:edge]], axis=1)
    second = jnp.concatenate([both[:, main:2 * main], both[:, edge:]], axis=1)
    return first, second


def halves(x):
    high = x.astype(BF16).astype(F32)
    return high, x - high


def lane_pad(parts):
    total = sum(p.shape[1] for p in parts)
    extra = -total % 128
    if extra:
        parts = parts + [jnp.zeros((parts[0].shape[0], extra), F32)]
    return jnp.concatenate(parts, axis=1).astype(BF16)


def row_pad(parts):
    total = sum(p.shape[0] for p in parts)
    extra = -total % 128
    if extra:
        parts = parts + [jnp.zeros((extra, parts[0].shape[1]), F32)]
    return jnp.concatenate(parts, axis=0).astype(BF16)


def left_operand(block):
    high, low = halves(block)
    return lane_pad([high, low, high])


def left_rows(rows):
    high, low = halves(rows)
    return row_pad([high, high, low])


def right_operand(main, tail):
    high, low = halves(main)
    end_high, end_low = halves(tail)
    return jnp.concatenate(
        [high.astype(BF16), low.astype(BF16), high.astype(BF16), lane_pad([end_high, end_low, end_high])],
        axis=1,
    )


def right_rows(block, main):
    high, low = halves(block)
    return row_pad(
        [high[:main], high[:main], low[:main], high[main:], high[main:], low[main:]]
    )


def dot(a, b):
    return jnp.dot(a, b, preferred_element_type=F32)


def kernel(
    energies, cells, offsets, orbitals, less_hbm, greater_hbm, vdiag_hbm, vup_hbm,
    diag_out, upper_out,
    less, greater, vdiag, vup, shifted, outgoing, polar, beside, v_out, v_in,
    left, right, a_sum, o_sum, diag, upper,
    in_sem, out_sem, swap_send, swap_recv, side_send, side_recv, v_send, v_recv,
):
    me = lax.axis_index("energy")
    cell = lax.axis_index("cell")
    rows, width = less.shape[2], less.shape[3]
    main = width // 128 * 128
    half = width // 2
    has_next = cell < cells - 1
    has_prev = cell > 0

    def peer(k):
        if energies & (energies - 1):
            return lax.rem(me + k, energies)
        other, bit = me, 1
        while bit <= k:
            if k & bit:
                other = other + bit * (1 - 2 * lax.rem(me // bit, 2))
            bit *= 2
        return other

    loads = [
        pltpu.make_async_copy(src, dst, in_sem.at[i])
        for i, (src, dst) in enumerate(
            [(vdiag_hbm, vdiag), (vup_hbm, vup), (less_hbm, less), (greater_hbm, greater)]
        )
    ]
    for load in loads:
        load.start()

    barrier = pltpu.get_barrier_semaphore()
    for k in range(1, energies):
        pl.semaphore_signal(barrier, inc=1, device_id=(peer(k), cell), device_id_type=MESH)

    @pl.when(has_next)
    def _():
        pl.semaphore_signal(barrier, inc=1, device_id=(me, cell + 1), device_id_type=MESH)

    @pl.when(has_prev)
    def _():
        pl.semaphore_signal(barrier, inc=1, device_id=(me, cell - 1), device_id_type=MESH)

    @pl.when(jnp.logical_not(has_prev))
    def _():
        beside[0] = jnp.zeros(beside.shape[1:], F32)
        v_in[0] = jnp.zeros(v_in.shape[1:], F32)

    @pl.when(jnp.logical_not(has_next))
    def _():
        beside[1] = jnp.zeros(beside.shape[1:], F32)
        v_in[1] = jnp.zeros(v_in.shape[1:], F32)

    late = lax.rem(cell, 2)
    early = 1 - late
    last = energies - 1

    def v_copy(side):
        return pltpu.make_async_remote_copy(
            src_ref=v_out.at[side], dst_ref=v_in.at[side],
            send_sem=v_send.at[side], recv_sem=v_recv.at[side],
            device_id=(me, cell + 1 - 2 * side), device_id_type=MESH,
        )

    cut_at = rows // 2 // 8 * 8

    def pieces(k):
        if k and k == last and cut_at:
            return [(0, pl.ds(0, cut_at)), (1, pl.ds(cut_at, rows - cut_at))]
        return [(0, pl.ds(0, rows))]

    def side_copy(side, k, piece, at):
        slot = slots[k]
        return pltpu.make_async_remote_copy(
            src_ref=polar.at[slot, at], dst_ref=beside.at[side, slot, at],
            send_sem=side_send.at[side, k, piece], recv_sem=side_recv.at[side, k, piece],
            device_id=(me, cell + 1 - 2 * side), device_id_type=MESH,
        )

    def side_copies(side, k):
        return [side_copy(side, k, piece, at) for piece, at in pieces(k)]

    def swap_copies(k):
        return [
            pltpu.make_async_remote_copy(
                src_ref=outgoing.at[peer(k), at], dst_ref=polar.at[me, at],
                send_sem=swap_send.at[k, piece], recv_sem=swap_recv.at[k, piece],
                device_id=(peer(k), cell), device_id_type=MESH,
            )
            for piece, at in pieces(k)
        ]

    def source(k):
        return peer(k if not energies & (energies - 1) else energies - k)

    slots = [me] + [source(k) for k in range(1, energies)]

    def swap_arrivals(k):
        return [
            pltpu.make_async_remote_copy(
                src_ref=outgoing.at[slots[k], at], dst_ref=polar.at[slots[k], at],
                send_sem=swap_send.at[k, piece], recv_sem=swap_recv.at[k, piece],
                device_id=(slots[k], cell), device_id_type=MESH,
            )
            for piece, at in pieces(k)
        ]

    def forward(k, piece, at):
        @pl.when(has_next)
        def _():
            side_copy(0, k, piece, at).start()

        @pl.when(has_prev)
        def _():
            side_copy(1, k, piece, at).start()

    here_orbitals = orbitals[cell]
    next_orbitals = jnp.where(has_next, orbitals[jnp.minimum(cell + 1, cells - 1)], 0)
    row = lax.broadcasted_iota(jnp.int32, (width, width), 0)
    col = lax.broadcasted_iota(jnp.int32, (width, width), 1)
    loads[0].wait()
    loads[1].wait()
    vd = jnp.where((row < here_orbitals) & (col < here_orbitals), vdiag[...], 0.0)
    vu = jnp.where((row < here_orbitals) & (col < next_orbitals), vup[...], 0.0)
    vdiag[...] = vd
    vup[...] = vu
    v_out[0] = pack(vu[:half], vu[half:], main)
    v_out[1] = pack(vd[:half], vd[half:], main)

    met = energies - 1 + jnp.where(has_next, 1, 0) + jnp.where(has_prev, 1, 0)
    pl.semaphore_wait(barrier, met)

    @pl.when(has_next)
    def _():
        v_copy(0).start()

    @pl.when(has_prev)
    def _():
        v_copy(1).start()

    loads[2].wait()
    loads[3].wait()
    scale = 1.0 / math.sqrt(energies)

    def polarize(step, carry):
        at = pl.ds(pl.multiple_of(step * 8, 8), 8)
        l_re = [less[0, m, at, :] for m in range(energies)]
        l_im = [less[1, m, at, :] for m in range(energies)]
        g_re = [greater[0, m, at, :] for m in range(energies)]
        g_im = [greater[1, m, at, :] for m in range(energies)]
        for shift in range(energies):
            real = imag = None
            for m in range(shift, energies):
                r = l_re[m] * g_re[m - shift] + l_im[m] * g_im[m - shift]
                i = l_im[m] * g_re[m - shift] - l_re[m] * g_im[m - shift]
                real = r if real is None else real + r
                imag = i if imag is None else imag + i
            shifted[shift, at, :] = pack(real * scale, imag * scale, main)
        return carry

    lax.fori_loop(0, rows // 8, polarize, 0)
    polar[me] = shifted[offsets[me]]
    forward(0, *pieces(0)[0])
    for k in range(1, energies):
        n = peer(k)
        outgoing[n] = shifted[offsets[n]]
        if k < last or last == 1:
            for copy in swap_copies(k):
                copy.start()

    def cut(which, block):
        for e in range(energies):
            left[which, e] = left_operand(block[:, e * rows:(e + 1) * rows])

    vd = vdiag[...]
    cut(HERE, vd)
    right[HERE] = right_rows(pack(vd.T, vup[...], main), main)
    cut(NEXT, vup[...])

    def add_left(which, slot, block, first):
        product = dot(left[which, slot], left_rows(block))
        if first:
            a_sum[which] = product
        else:
            a_sum[which] += product

    def split(which):
        a = a_sum[which]
        edge = 2 * main + width - main
        return (
            right_operand(a[:, :main], a[:, 2 * main:edge]),
            right_operand(a[:, main:2 * main], a[:, edge:]),
        )

    def arrive(k):
        for copy, (piece, at) in zip(swap_arrivals(k), pieces(k)):
            copy.wait_recv()
            forward(k, piece, at)

    def take_here(k):
        add_left(HERE, slots[k], polar[slots[k]], k == 0)

    def take_side(side, k):
        @pl.when(jnp.where(side == 0, has_prev, has_next))
        def _():
            for copy in side_copies(side, k):
                copy.wait_recv()

        add_left(2 - side, slots[k], beside[side, slots[k]], k == 0)

    def take_right(which, first):
        for part, operand in enumerate(split(which)):
            product = dot(operand, right[which])
            if first:
                o_sum[part] = product
            else:
                o_sum[part] += product

    take_here(0)
    for k in range(1, last):
        arrive(k)
    if last > 1:
        for k in range(1, last):
            for copy in swap_copies(k):
                copy.wait_send()
        for copy in swap_copies(last):
            copy.start()
    for k in range(1, last):
        take_here(k)

    @pl.when(has_prev)
    def _():
        v_copy(0).wait_recv()

    @pl.when(has_next)
    def _():
        v_copy(1).wait_recv()

    def whole(side):
        top, bottom = unpack(v_in[side], main, width)
        return jnp.concatenate([top, bottom], axis=0)

    vp = whole(0)
    cut(PREV, vp.T)
    right[PREV] = right_rows(pack(vp, jnp.zeros_like(vp), main), main)
    vn = whole(1)
    right[NEXT] = right_rows(pack(vup[...].T, vn.T, main), main)

    for k in range(last):
        take_side(early, k)
        if k < last - 1:
            take_side(late, k)
    if last:
        arrive(last)
        take_here(last)
    take_right(HERE, True)
    if last:
        take_side(late, last - 1)
    take_side(early, last)
    take_right(2 - early, False)
    take_side(late, last)
    writes = []
    for part, operand in enumerate(split(2 - late)):
        total = o_sum[part] + dot(operand, right[2 - late])
        diag[part], upper[part] = unpack(total, main, width)
        for i, (src, dst) in enumerate([(diag, diag_out), (upper, upper_out)]):
            writes.append(pltpu.make_async_copy(src.at[part], dst.at[part], out_sem.at[i, part]))
            writes[-1].start()

    for copy in swap_copies(last) if last else []:
        copy.wait_send()

    @pl.when(has_next)
    def _():
        v_copy(0).wait_send()
        for k in range(energies):
            for copy in side_copies(0, k):
                copy.wait_send()

    @pl.when(has_prev)
    def _():
        v_copy(1).wait_send()
        for k in range(energies):
            for copy in side_copies(1, k):
                copy.wait_send()

    for write in writes:
        write.wait()


def deliver(diag_in, upper_in, diag, upper, held, in_sem, out_sem):
    rows = diag_in.shape[1]
    middle = rows // 16 * 8
    copies = []
    for i, (src, dst) in enumerate([(diag_in, diag), (upper_in, upper)]):
        for part in range(2):
            for j, at in enumerate([pl.ds(0, middle), pl.ds(middle, rows - middle)]):
                here = held.at[i, part, at]
                copies.append((
                    pltpu.make_async_copy(src.at[part, at], here, in_sem.at[i, part, j]),
                    pltpu.make_async_copy(here, dst.at[part, at], out_sem.at[i, part, j]),
                ))
    for arriving, _ in copies:
        arriving.start()
    for arriving, leaving in copies:
        arriving.wait()
        leaving.start()
    for _, leaving in copies:
        leaving.wait()


def solution(mesh):
    energies, cells = mesh.shape["energy"], mesh.shape["cell"]

    def per_device(green_less, green_greater, offsets, orbitals, coulomb_diag, coulomb_up):
        less = jnp.squeeze(green_less, 2)
        greater = jnp.squeeze(green_greater, 2)
        rows, width = less.shape[2], less.shape[3]
        main = width // 128 * 128
        depth = 3 * rows + -3 * rows % 128
        long = 3 * width + -3 * width % 128
        shape = jax.ShapeDtypeStruct((2, width, width), F32)
        anywhere = pl.BlockSpec(memory_space=pltpu.HBM)
        scalars = pl.BlockSpec(memory_space=pltpu.SMEM)
        dma = pltpu.SemaphoreType.DMA
        products = width * width * width * 2 * 8 * 3
        diag, upper = pl.pallas_call(
            functools.partial(kernel, energies, cells),
            out_shape=(shape, shape),
            in_specs=[scalars, scalars, anywhere, anywhere, anywhere, anywhere],
            out_specs=(anywhere, anywhere),
            scratch_shapes=[
                pltpu.VMEM(less.shape, F32),
                pltpu.VMEM(less.shape, F32),
                pltpu.VMEM((width, width), F32),
                pltpu.VMEM((width, width), F32),
                pltpu.VMEM((energies, rows, 2 * width), F32),
                pltpu.VMEM((energies, rows, 2 * width), F32),
                pltpu.VMEM((energies, rows, 2 * width), F32),
                pltpu.VMEM((2, energies, rows, 2 * width), F32),
                pltpu.VMEM((2, width // 2, 2 * width), F32),
                pltpu.VMEM((2, width // 2, 2 * width), F32),
                pltpu.VMEM((3, energies, width, depth), BF16),
                pltpu.VMEM((3, long, 2 * width), BF16),
                pltpu.VMEM((3, width, 2 * width), F32),
                pltpu.VMEM((2, width, 2 * width), F32),
                pltpu.VMEM((2, width, width), F32),
                pltpu.VMEM((2, width, width), F32),
                dma((4,)),
                dma((2, 2)),
                dma((energies, 2)),
                dma((energies, 2)),
                dma((2, energies, 2)),
                dma((2, energies, 2)),
                dma((2,)),
                dma((2,)),
            ],
            compiler_params=pltpu.CompilerParams(
                collective_id=0, has_side_effects=True, vmem_limit_bytes=62914560
            ),
            cost_estimate=pl.CostEstimate(
                flops=2 * products, bytes_accessed=4 * less.size * 4, transcendentals=0
            ),
            name="screen",
        )(offsets, orbitals, less, greater, coulomb_diag[0], coulomb_up[0])
        diag, upper = pl.pallas_call(
            deliver,
            out_shape=(shape, shape),
            in_specs=[pl.BlockSpec(memory_space=pl.ANY)] * 2,
            out_specs=(pl.BlockSpec(memory_space=pl.ANY),) * 2,
            scratch_shapes=[pltpu.VMEM((2,) + shape.shape, F32), dma((2, 2, 2)), dma((2, 2, 2))],
            cost_estimate=pl.CostEstimate(
                flops=0, bytes_accessed=16 * width * width * 2, transcendentals=0
            ),
            compiler_params=pltpu.CompilerParams(vmem_limit_bytes=60 * 1024 * 1024),
            name="deliver",
        )(diag, upper)
        return diag[:, None, None], upper[:, None, None]

    in_specs = (
        P(None, None, "cell", "energy", None),
        P(None, None, "cell", "energy", None),
        P(),
        P(),
        P("cell", None, None),
        P("cell", None, None),
    )
    out_specs = (P(None, "energy", "cell", None, None), P(None, "energy", "cell", None, None))
    return jax.shard_map(
        per_device, mesh=mesh, in_specs=in_specs, out_specs=out_specs, check_vma=False
    )
```
